256 devices in a mesh: row: 32 (over z_lo, x, core), col: 8 (over y, z_hi).
Axes of the slice: x: 4, y: 4, z: 8 (z_hi: 2, z_lo: 4; z = z_hi * 4 + z_lo), core: 2. Of those that a mesh axis runs over, the one named last changes fastest.
Arguments:
- c_panel: float32 [16384, 128], P('row', 'col'), may hold values from -0.046875 to 0.046875
- cbar_in: float32 [16384, 128], P('row', 'col'), may hold values from -6 to 6
- factor_diagonal_block: float32 [128, 128], replicated, may hold values from -0.9 to 4, as said below
- dbar_in: float32 [128, 128], replicated, may hold values from -6 to 6
- r_panel: float32 [128, 16384], P('row', 'col'), may hold values from -0.6 to 0.6
- rbar_in: float32 [128, 16384], P('row', 'col'), may hold values from -6 to 6
- b_block: float32 [16384, 16384], P('row', 'col'), may hold values from -0.046875 to 0.046875
- bbar_in: float32 [16384, 16384], P('row', 'col'), may hold values from -6 to 6
Outputs:
- cbar_out: float32 [16384, 128], P('row', 'col')
- bbar_out: float32 [16384, 16384], P('row', 'col')
- kernel_diagonal_adjoint: float32 [128, 128], P('row', 'col')
- rbar_out: float32 [128, 16384], P('row', 'col')
The draws below stay inside these ranges and needn't reach their ends.
Inputs may be any that keep to these rules, and one draw needn't show every extreme that they name: factor_diagonal_block is lower triangular; its diagonal entries lie in 2 to 4 and its entries below the diagonal in -0.9 to 0.9.
All inputs are finite; a program needn't handle non-finite values.
Results may differ from the reference program's by a relative error of at most 0.00007.
Values sent between devices are 32-bit elements; how exact they have to be, the bound alone decides.
A program may use at most 64 MiB of HBM per device.

```python
import jax
import jax.numpy as jnp
from jax import lax

NB = 128
M = 16384
J = 16384


def draw_factor_diagonal_block(key, part):
    key = jax.random.fold_in(key, 7)
    first, second = jax.random.split(key)
    diag_vals = jax.random.uniform(first, (NB,), jnp.float32, 2.0, 4.0)
    lower_vals = jnp.clip(jax.random.normal(second, (NB, NB), jnp.float32) * 0.15, -0.9, 0.9)
    return jnp.tril(lower_vals, -1) + jnp.diag(diag_vals)


def level_of(key, dims, cuts, smallest, top_value):
    def one(position, parts):
        steps = jax.random.uniform(jax.random.fold_in(jax.random.fold_in(key, 6), position), (parts,), jnp.float32, smallest / len(cuts), top_value / len(cuts))
        return jnp.repeat(jnp.exp(steps), dims[position] // parts).reshape((-1,) + (1,) * (len(dims) - position - 1))

    loudness = one(*cuts[0])
    for cut in cuts[1:]:
        loudness = loudness * one(*cut)
    return loudness


def gaussian(key, shape, width, limit, pieces=(), kind=jnp.bfloat16):
    loudness = level_of(key, shape, pieces, -0.22, 0.18) if pieces else 1.0
    result = jax.random.normal(key, shape, jnp.float32) * width * loudness
    return jnp.minimum(jnp.maximum(result, -limit), limit).astype(kind)


def setup_inputs(seed: int = 0) -> dict:
    keys = jax.random.split(jax.random.key(seed), 9)
    return {
        "c_panel": gaussian(keys[0], (M, NB), M ** -0.5, 0.046875, ((0, 32), (1, 8)), jnp.float32),
        "cbar_in": gaussian(keys[1], (M, NB), 1.0, 6.0, ((0, 32), (1, 8)), jnp.float32),
        "factor_diagonal_block": draw_factor_diagonal_block(jax.random.fold_in(keys[8], 71), 0),
        "dbar_in": gaussian(keys[3], (NB, NB), 1.0, 6.0, (), jnp.float32),
        "r_panel": gaussian(keys[4], (NB, J), 0.1, 0.6, ((0, 32), (1, 8)), jnp.float32),
        "rbar_in": gaussian(keys[5], (NB, J), 1.0, 6.0, ((0, 32), (1, 8)), jnp.float32),
        "b_block": gaussian(keys[6], (M, J), M ** -0.5, 0.046875, ((0, 32), (1, 8)), jnp.float32),
        "bbar_in": gaussian(keys[7], (M, J), 1.0, 6.0, ((0, 32), (1, 8)), jnp.float32),
    }


def lower_half_term(matrix):
    return jnp.tril(matrix) - 0.5 * jnp.diag(jnp.diag(matrix))

def reference(c_panel, cbar_in, factor_diagonal_block, dbar_in, r_panel, rbar_in, b_block, bbar_in):
    highest = lax.Precision.HIGHEST
    cbar_out = jax.scipy.linalg.solve_triangular(factor_diagonal_block, cbar_in.T, lower=True, trans='T').T
    bbar_out = bbar_in - jnp.dot(cbar_out.astype(jnp.float32), r_panel.astype(jnp.float32), precision=highest, preferred_element_type=jnp.float32)
    diagonal_adjoint_middle = dbar_in - jnp.tril(jnp.dot(cbar_out.T.astype(jnp.float32), c_panel.astype(jnp.float32), precision=highest, preferred_element_type=jnp.float32))
    proj = lower_half_term(jnp.dot(factor_diagonal_block.T.astype(jnp.float32), diagonal_adjoint_middle.astype(jnp.float32), precision=highest, preferred_element_type=jnp.float32))
    left_product_term = jax.scipy.linalg.solve_triangular(factor_diagonal_block, proj, lower=True, trans='T')
    sandwich_product = jax.scipy.linalg.solve_triangular(factor_diagonal_block, left_product_term.T, lower=True, trans='T').T
    kernel_diagonal_adjoint = lower_half_term(sandwich_product + sandwich_product.T)
    rbar_out = rbar_in - jnp.dot(cbar_out.T.astype(jnp.float32), b_block.astype(jnp.float32), precision=highest, preferred_element_type=jnp.float32)
    rbar_out = rbar_out - jnp.dot((kernel_diagonal_adjoint + kernel_diagonal_adjoint.T).astype(jnp.float32), r_panel.astype(jnp.float32), precision=highest, preferred_element_type=jnp.float32)
    return (cbar_out, bbar_out, kernel_diagonal_adjoint, rbar_out)
```

```python
import functools

import jax
import jax.numpy as jnp
from jax import lax
from jax.experimental import pallas as pl
from jax.experimental.pallas import tpu as pltpu
from jax.sharding import PartitionSpec as P

F32 = jnp.float32
BF16 = jnp.bfloat16
HI = lax.Precision.HIGHEST
MESH = pl.DeviceIdType.MESH
ANY = pl.ANY
NX, NZ, NY, NC, NH = 4, 4, 4, 2, 2
CH = 4
CW = 512


def dot(a, b, contract=((1,), (0,)), precision=HI):
    return lax.dot_general(
        a, b, (contract, ((), ())), precision=precision, preferred_element_type=F32
    )


def split(a):
    high = a.astype(BF16)
    return high, (a - high.astype(F32)).astype(BF16)


def kernel(
    c_hbm, cbar_hbm, l_hbm, d_hbm, r_hbm, rbar_hbm, b_hbm, bbar_hbm,
    cbar_out, bbar_out, kda_out, rbar_out,
    l_v, d_v, c_v, rbar_v, b_v, bbar_v, bh_v, bl_v,
    cg, rg, w_v, wp_v, x3_v, rh_v, rl_v,
    tb, tc, ts, xo, xd, xs, xa, zs, zr,
    ms, ma, mt, mb, mg,
    co_v, kd_v, ro_v,
    lsem, bsem, osem,
    cgs, cgr, rs, rr, tss, trs, xss, xrs, zss, zrs, mss, mrs,
):
    row, col = lax.axis_index("row"), lax.axis_index("col")
    core, x, zl = row % NC, (row // NC) % NX, row // (NC * NX)
    y, zh = col // NH, col % NH

    def dev(dz=0, dx=0, fc=0, dy=0, fz=0):
        c2 = 1 - core if fc else core
        h2 = 1 - zh if fz else zh
        z2, x2, y2 = (zl + dz) % NZ, (x + dx) % NX, (y + dy) % NY
        return (z2 * (NX * NC) + x2 * NC + c2, y2 * NH + h2)

    xc = [(dx, fc) for dx in range(NX) for fc in range(NC)][1:]
    zz = [(dz, fz) for dz in range(NZ) for fz in range(NH)][1:]
    peers = [dev(dx=dx, fc=fc) for dx, fc in xc]
    peers += [dev(dz=dz, fz=fz) for dz, fz in zz]
    peers += [dev(dy=dy) for dy in range(1, NY)]

    barrier = pltpu.get_barrier_semaphore()
    for peer in peers:
        pl.semaphore_signal(barrier, inc=1, device_id=peer, device_id_type=MESH)

    def local(src, dst, sem):
        copy = pltpu.make_async_copy(src, dst, sem)
        copy.start()
        return copy

    sent = []

    def send(src, dst, ssem, rsem, to):
        copy = pltpu.make_async_remote_copy(
            src_ref=src, dst_ref=dst, send_sem=ssem, recv_sem=rsem,
            device_id=to, device_id_type=MESH,
        )
        copy.start()
        sent.append(copy)
        return copy

    my_slot = core * (NX * NZ) + x * NZ + zl
    l_c = local(l_hbm, l_v, lsem.at[0])
    cg_c = local(cbar_hbm, cg.at[col], lsem.at[1])
    c_c = local(c_hbm, c_v, lsem.at[2])
    r_c = local(r_hbm, rg.at[my_slot], lsem.at[3])
    d_c = local(d_hbm, d_v, lsem.at[4])
    rb_c = local(rbar_hbm, rbar_v, lsem.at[5])
    b_c = [
        local(b_hbm.at[:, pl.ds(k * CW, CW)], b_v.at[:, pl.ds(k * CW, CW)], bsem.at[k])
        for k in range(CH)
    ]
    bb_c = local(bbar_hbm, bbar_v, lsem.at[6])

    pl.semaphore_wait(barrier, len(peers))

    mine = cg.at[col]
    cz = send(cbar_hbm, mine, cgs.at[0], cgr.at[0], dev(fz=1))
    cy = [
        send(cbar_hbm, mine, cgs.at[dy], cgr.at[dy], dev(dy=dy)) for dy in range(1, NY)
    ]
    rz = [
        send(r_hbm, rg.at[my_slot], rs.at[dz - 1], rr.at[dz - 1], dev(dz=dz))
        for dz in range(1, NZ)
    ]

    rows = lax.broadcasted_iota(jnp.int32, (128, 128), 0)
    cols = lax.broadcasted_iota(jnp.int32, (128, 128), 1)
    l_c.wait()
    u = l_v[...].T
    eye = rows == cols
    w = jnp.where(eye, 1.0 / jnp.where(eye, u, 1.0), 0.0)

    def level(w, s):
        mask = (rows // (2 * s) == cols // (2 * s)) & (rows % (2 * s) < s) & (cols % (2 * s) >= s)
        return w - dot(dot(w, jnp.where(mask, u, 0.0)), w)

    for s in (1, 2, 4):
        w = level(w, s)

    cz.wait_recv()
    part = cg.at[y * NH + 1 - zh]
    cy += [
        send(part, part, cgs.at[3 + dy], cgr.at[3 + dy], dev(dy=dy)) for dy in range(1, NY)
    ]

    for copy in rz:
        copy.wait_recv()
    r_c.wait()

    def group(g):
        return rg.at[pl.ds(core * (NX * NZ) + ((x + g) % NX) * NZ, NZ)]

    own = group(0)
    r_right = send(own, own, rs.at[3], rr.at[3], dev(dx=1))
    r_left = send(own, own, rs.at[4], rr.at[4], dev(dx=3))
    r_core = [send(own, own, rs.at[5], rr.at[5], dev(fc=1))]

    for s in (8, 16, 32, 64):
        w = level(w, s)
    w_v[...] = w
    natural = (rows % 16) // 4 * 32 + (rows // 16) % 4 * 8 + rows // 64 * 4 + rows % 4
    wp = dot(jnp.where(cols == natural, 1.0, 0.0), w)
    wp_v[...] = wp

    for k in range(CH):
        b_c[k].wait()
        high, low = split(b_v[:, k * CW : (k + 1) * CW])
        bh_v[:, k * CW : (k + 1) * CW] = high
        bl_v[:, k * CW : (k + 1) * CW] = low

    for copy in cy:
        copy.wait_recv()
    cg_c.wait()
    ct = cg[...].reshape(128, 512)

    c_c.wait()
    ms[...] = dot(c_v[...], ct, ((1,), (1,)))
    m_x = [
        send(ms, ma.at[i], mss.at[i], mrs.at[i], dev(dx=dx, fc=fc))
        for i, (dx, fc) in enumerate(xc)
    ]

    ctn = dot(wp, ct)
    nh, nl = split(ctn)
    both = jnp.concatenate([nh, nl], axis=0)

    def chunk(k):
        where = slice(k * CW, (k + 1) * CW)
        p = dot(both, bh_v[:, where], precision=None)
        t = p[:128] + p[128:] + dot(nh, bl_v[:, where], precision=None)
        tb[k, 0] = t[:64]
        tb[k, 1] = t[64:]
        return send(tb.at[k, 1 - core], tc.at[k], tss.at[k], trs.at[k], dev(fc=1))

    t_core = []
    x_opp = []
    x_dir = []
    x_acc = []

    def after_core(k):
        t_core[k].wait_recv()
        v = tb[k, core] + tc[k]
        for q in range(NX):
            ts[k, q] = v[16 * q : 16 * (q + 1)]
        step = 1 if k % 2 == 0 else 3
        x_opp.append(
            send(ts.at[k, (x + 2) % NX], xo.at[k], xss.at[k, 0], xrs.at[k, 0], dev(dx=step))
        )
        x_dir.append(
            send(ts.at[k, (x - step + NX) % NX], xd.at[k], xss.at[k, 1], xrs.at[k, 1], dev(dx=4 - step))
        )

    t_core.append(chunk(0))

    total = ms[...]
    for i, copy in enumerate(m_x):
        copy.wait_recv()
        total = total + ma[i]
    mt[...] = total
    m_z = [
        send(mt, mb.at[i], mss.at[7 + i], mrs.at[7 + i], dev(dz=dz, fz=fz))
        for i, (dz, fz) in enumerate(zz)
    ]

    t_core.append(chunk(1))
    after_core(0)
    t_core.append(chunk(2))
    after_core(1)
    t_core.append(chunk(3))
    after_core(2)
    after_core(3)

    r_right.wait_recv()
    r_left.wait_recv()
    from_left, from_right = group(3), group(1)
    half_a = from_left.at[:, :, pl.ds(0, 1024)]
    half_b = from_right.at[:, :, pl.ds(1024, 1024)]
    r_fa = send(half_a, half_a, rs.at[6], rr.at[6], dev(dx=1))
    r_fb = send(half_b, half_b, rs.at[7], rr.at[7], dev(dx=3))
    r_core.append(send(from_left, from_left, rs.at[8], rr.at[8], dev(fc=1)))
    r_core.append(send(from_right, from_right, rs.at[9], rr.at[9], dev(fc=1)))

    for k in range(CH):
        step = 1 if k % 2 == 0 else 3
        x_opp[k].wait_recv()
        xs[k] = ts[k, (x + step) % NX] + xo[k]
        x_acc.append(send(xs.at[k], xa.at[k], xss.at[k, 2], xrs.at[k, 2], dev(dx=step)))

    same, other = mt[...], None
    for i, (dz, fz) in enumerate(zz):
        m_z[i].wait_recv()
        if fz:
            other = mb[i] if other is None else other + mb[i]
        else:
            same = same + mb[i]
    mg[col] = same
    mg[y * NH + 1 - zh] = other
    pair = mg.at[pl.ds(y * NH, NH)]
    m_y = [
        send(pair, pair, mss.at[13 + dy], mrs.at[13 + dy], dev(dy=dy)) for dy in range(1, NY)
    ]

    co_v[...] = dot(w_v[pl.ds(pl.multiple_of(col * 16, 16), 16), :], ct)
    o_c = [local(co_v, cbar_out, osem.at[0])]

    r_fa.wait_recv()
    r_fb.wait_recv()
    across = group(2)
    r_core.append(send(across, across, rs.at[10], rr.at[10], dev(fc=1)))

    z_all = []
    for k in range(CH):
        x_dir[k].wait_recv()
        x_acc[k].wait_recv()
        v = ts[k, x] + xd[k] + xa[k]
        for q in range(NZ):
            zs[k, q] = v[4 * q : 4 * q + 4]
        z_all.append([
            send(zs.at[k, (zl + dz) % NZ], zr.at[k, dz - 1], zss.at[k, dz - 1], zrs.at[k, dz - 1], dev(dz=dz))
            for dz in range(1, NZ)
        ])

    for copy in r_core:
        copy.wait_recv()
    for p in range(8):
        v = jnp.concatenate([rg[4 * p + q] for q in range(4)], axis=0)
        high, low = split(v)
        rh_v[16 * p : 16 * (p + 1), :] = high
        rl_v[16 * p : 16 * (p + 1), :] = low

    cn = ctn.T
    ch, cl = split(cn)
    x3_v[...] = jnp.concatenate([ch, cl, ch], axis=1)
    bb_c.wait()
    for k in range(CH):
        where = slice(k * CW, (k + 1) * CW)
        r3 = jnp.concatenate([rh_v[:, where], rh_v[:, where], rl_v[:, where]], axis=0)
        bbar_v[:, where] = bbar_v[:, where] - dot(x3_v[...], r3, precision=None)
        o_c.append(
            local(bbar_v.at[:, pl.ds(k * CW, CW)], bbar_out.at[:, pl.ds(k * CW, CW)], osem.at[3 + k])
        )

    for copy in m_y:
        copy.wait_recv()
    d_c.wait()
    mt_full = mg[...].reshape(128, 128)
    product = dot(w_v[...], mt_full, ((1,), (1,)))
    mid = d_v[...] - jnp.where(rows >= cols, product, 0.0)
    z = dot(l_v[...].T, mid)
    q = jnp.where(rows >= cols, z, z.T)
    w8 = w_v[pl.ds(pl.multiple_of(row // 2 * 8, 8), 8), :]
    wq = dot(w8, q)
    a8 = dot(wq, w_v[...], ((1,), (1,)))
    a4 = jnp.where(core == 0, a8[:4], a8[4:])
    row4 = lax.broadcasted_iota(jnp.int32, (4, 128), 0) + row * 4
    col4 = lax.broadcasted_iota(jnp.int32, (4, 128), 1)
    kda = jnp.where(row4 > col4, a4, jnp.where(row4 == col4, 0.5 * a4, 0.0))
    pick = lax.broadcasted_iota(jnp.int32, (128, 16), 0) == (
        lax.broadcasted_iota(jnp.int32, (128, 16), 1) + col * 16
    )
    kd_v[...] = dot(kda, jnp.where(pick, 1.0, 0.0))
    o_c.append(local(kd_v, kda_out, osem.at[1]))

    ap = dot(wq, wp_v[...], ((1,), (1,)))
    ah, al = split(ap)
    a3 = jnp.concatenate([ah, al, ah], axis=1)
    for k in range(CH):
        where = slice(k * CW, (k + 1) * CW)
        r3 = jnp.concatenate([rh_v[:, where], rh_v[:, where], rl_v[:, where]], axis=0)
        corr = dot(a3, r3, precision=None)
        corr = jnp.where(core == 0, corr[:4], corr[4:])
        acc = zs[k, zl]
        for dz in range(1, NZ):
            z_all[k][dz - 1].wait_recv()
            acc = acc + zr[k, dz - 1]
        ro_v[:, where] = rbar_v_read(rb_c, rbar_v, k, where) - acc - corr
    o_c.append(local(ro_v, rbar_out, osem.at[2]))

    for copy in o_c:
        copy.wait()
    for copy in sent:
        copy.wait_send()


def rbar_v_read(copy, ref, k, where):
    if k == 0:
        copy.wait()
    return ref[:, where]


def body(c_panel, cbar_in, factor, dbar_in, r_panel, rbar_in, b_block, bbar_in):
    vmem = pltpu.VMEM
    sem = pltpu.SemaphoreType.DMA
    scratch = [
        vmem((128, 128), F32), vmem((128, 128), F32), vmem((16, 512), F32), vmem((4, 2048), F32),
        vmem((512, 2048), F32), vmem((512, 2048), F32), vmem((512, 2048), BF16), vmem((512, 2048), BF16),
        vmem((8, 16, 512), F32), vmem((32, 4, 2048), F32), vmem((128, 128), F32), vmem((128, 128), F32),
        vmem((512, 384), BF16), vmem((128, 2048), BF16), vmem((128, 2048), BF16),
        vmem((CH, 2, 64, CW), F32), vmem((CH, 64, CW), F32), vmem((CH, NX, 16, CW), F32),
        vmem((CH, 16, CW), F32), vmem((CH, 16, CW), F32), vmem((CH, 16, CW), F32), vmem((CH, 16, CW), F32),
        vmem((CH, NZ, 4, CW), F32), vmem((CH, NZ - 1, 4, CW), F32),
        vmem((16, 128), F32), vmem((7, 16, 128), F32), vmem((16, 128), F32), vmem((7, 16, 128), F32),
        vmem((8, 16, 128), F32),
        vmem((16, 512), F32), vmem((4, 16), F32), vmem((4, 2048), F32),
        sem((7,)), sem((CH,)), sem((3 + CH,)),
        sem((7,)), sem((7,)), sem((11,)), sem((11,)), sem((CH,)), sem((CH,)),
        sem((CH, 3)), sem((CH, 3)), sem((CH, 3)), sem((CH, 3)), sem((17,)), sem((17,)),
    ]
    cbar_t, bbar_out, kda, rbar_out = pl.pallas_call(
        kernel,
        out_shape=(
            jax.ShapeDtypeStruct((16, 512), F32),
            jax.ShapeDtypeStruct((512, 2048), F32),
            jax.ShapeDtypeStruct((4, 16), F32),
            jax.ShapeDtypeStruct((4, 2048), F32),
        ),
        in_specs=[pl.BlockSpec(memory_space=ANY)] * 8,
        out_specs=[pl.BlockSpec(memory_space=ANY)] * 4,
        scratch_shapes=scratch,
        compiler_params=pltpu.CompilerParams(
            collective_id=0, has_side_effects=True, vmem_limit_bytes=56 * 1024 * 1024
        ),
        name="block_step",
    )(c_panel.T, cbar_in.T, factor, dbar_in, r_panel, rbar_in, b_block, bbar_in)
    return cbar_t.T, bbar_out, kda, rbar_out


def solution(mesh):
    spec = P("row", "col")
    in_specs = (spec, spec, P(), P(), spec, spec, spec, spec)
    return jax.shard_map(
        body, mesh=mesh, in_specs=in_specs, out_specs=(spec,) * 4, check_vma=False
    )
```

```python
import jax
import jax.numpy as jnp
from jax import lax
from jax.experimental import pallas as pl
from jax.experimental.pallas import tpu as pltpu
from jax.sharding import PartitionSpec as P

F32 = jnp.float32
BF16 = jnp.bfloat16
HI = lax.Precision.HIGHEST
MESH = pl.DeviceIdType.MESH
NX, NZ, NY, NC, NH = 4, 4, 4, 2, 2
CH = 4
CW = 512


def dot(a, b, contract=((1,), (0,)), precision=HI):
    return lax.dot_general(
        a, b, (contract, ((), ())), precision=precision, preferred_element_type=F32
    )


def split(a):
    high = a.astype(BF16)
    return high, (a - high.astype(F32)).astype(BF16)


def kernel(
    c_hbm, cbar_hbm, l_hbm, d_hbm, r_hbm, rbar_hbm, b_hbm, bbar_hbm,
    cbar_out, bbar_out, kda_out, rbar_out,
    l_v, d_v, cc, rbar_v, b_v, bbar_v, bh_v, bl_v,
    cg, rg, w_v, wk_v, wp_v, x3_v, rh_v, rl_v,
    tb, tc, ts, xr, zs, zr,
    ms, ma, mt, mb, mg,
    lsem, bsem,
    cgs, cgr, rs, rr, tss, trs, xss, xrs, zss, zrs, mss, mrs,
):
    row, col = lax.axis_index("row"), lax.axis_index("col")
    core, x, zl = row % NC, (row // NC) % NX, row // (NC * NX)
    y, zh = col // NH, col % NH

    def dev(dz=0, dx=0, fc=0, dy=0, fz=0):
        c2 = 1 - core if fc else core
        h2 = 1 - zh if fz else zh
        z2, x2, y2 = (zl + dz) % NZ, (x + dx) % NX, (y + dy) % NY
        return (z2 * (NX * NC) + x2 * NC + c2, y2 * NH + h2)

    xc = [(dx, fc) for dx in range(NX) for fc in range(NC)][1:]
    zz = [(dz, fz) for dz in range(NZ) for fz in range(NH)][1:]
    peers = [dev(dz=dz, fz=fz) for dz, fz in reversed(zz)]
    peers += [dev(dy=dy) for dy in (2, 1, 3)]
    peers += [dev(dx=dx, fc=fc) for dx, fc in xc]

    barrier = pltpu.get_barrier_semaphore()
    for peer in peers:
        pl.semaphore_signal(barrier, inc=1, device_id=peer, device_id_type=MESH)

    pending = []

    def local(src, dst, sem):
        copy = pltpu.make_async_copy(src, dst, sem)
        copy.start()
        pending.append(copy)
        return copy

    def landed(copy):
        copy.wait()
        pending[:] = [other for other in pending if other is not copy]

    sent = []

    def send(src, dst, ssem, rsem, to):
        copy = pltpu.make_async_remote_copy(
            src_ref=src, dst_ref=dst, send_sem=ssem, recv_sem=rsem,
            device_id=to, device_id_type=MESH,
        )
        copy.start()
        sent.append(copy)
        return copy

    def end():
        for copy in pending:
            copy.wait()
        for copy in sent:
            copy.wait_send()

    my_slot = core * (NX * NZ) + x * NZ + zl
    l_c = local(l_hbm, l_v, lsem.at[0])
    cg_c = local(cbar_hbm, cg.at[zh, y], lsem.at[1])
    c_c = local(c_hbm, cc.at[zh], lsem.at[2])
    r_c = local(r_hbm, rg.at[my_slot], lsem.at[3])
    d_c = local(d_hbm, d_v, lsem.at[4])
    rb_c = local(rbar_hbm, rbar_v, lsem.at[5])
    b_c = [
        local(b_hbm.at[:, pl.ds(k * CW, CW)], b_v.at[:, pl.ds(k * CW, CW)], bsem.at[k])
        for k in range(CH)
    ]
    bb_c = local(bbar_hbm, bbar_v, lsem.at[6])

    pl.semaphore_wait(barrier, len(peers))

    cz = send(cbar_hbm, cg.at[zh, y], cgs.at[0], cgr.at[0], dev(fz=1))
    cc_z = send(c_hbm, cc.at[zh], cgs.at[7], cgr.at[7], dev(fz=1))
    cy = [
        send(cbar_hbm, cg.at[zh, y], cgs.at[dy], cgr.at[dy], dev(dy=dy)) for dy in (2, 1, 3)
    ]
    rz = [
        send(r_hbm, rg.at[my_slot], rs.at[dz - 1], rr.at[dz - 1], dev(dz=dz))
        for dz in range(1, NZ)
    ]

    rows = lax.broadcasted_iota(jnp.int32, (128, 128), 0)
    cols = lax.broadcasted_iota(jnp.int32, (128, 128), 1)
    landed(l_c)
    u = l_v[...].T
    eye = rows == cols
    w = jnp.where(eye, 1.0 / jnp.where(eye, u, 1.0), 0.0)
    for s in (1, 2, 4, 8, 16, 32, 64):
        mask = (rows // (2 * s) == cols // (2 * s)) & (rows % (2 * s) < s) & (cols % (2 * s) >= s)
        w = w - dot(dot(w, jnp.where(mask, u, 0.0)), w)
    w_v[...] = w

    cz.wait_recv()
    part = cg.at[1 - zh, y]
    cy2 = [send(part, part, cgs.at[3 + dy], cgr.at[3 + dy], dev(dy=dy)) for dy in (2, 1, 3)]

    for copy in cy:
        copy.wait_recv()
    cc_z.wait_recv()
    landed(cg_c)
    landed(c_c)
    pt = dot(cc[...].reshape(32, 512), cg[zh].reshape(64, 512), ((1,), (1,)))
    ms[...] = jnp.concatenate([pt[:16], pt[16:]], axis=1)
    m_x = [
        send(ms, ma.at[i], mss.at[i], mrs.at[i], dev(dx=dx, fc=fc))
        for i, (dx, fc) in enumerate(xc)
    ]

    for copy in rz:
        copy.wait_recv()
    landed(r_c)

    def group(g):
        return rg.at[pl.ds(core * (NX * NZ) + ((x + g) % NX) * NZ, NZ)]

    own = group(0)
    r_x = [send(own, own, rs.at[2 + dx], rr.at[2 + dx], dev(dx=dx)) for dx in (2, 1, 3)]
    r_core = [send(own, own, rs.at[6], rr.at[6], dev(fc=1))]

    natural = ((cols % 64) // 16 * 2 + cols // 64) * 16 + cols % 16
    wk = dot(w, jnp.where(rows == natural, 1.0, 0.0))
    wk_v[...] = wk
    natural = (rows % 16) // 4 * 32 + (rows // 16) % 4 * 8 + rows // 64 * 4 + rows % 4
    order = jnp.where(cols == natural, 1.0, 0.0)
    wp_v[...] = dot(order, w)
    wpk = dot(order, wk)

    for k in range(CH):
        landed(b_c[k])
        high, low = split(b_v[:, k * CW : (k + 1) * CW])
        bh_v[:, k * CW : (k + 1) * CW] = high
        bl_v[:, k * CW : (k + 1) * CW] = low

    for copy in cy2:
        copy.wait_recv()
    ct = cg[...].reshape(128, 512)
    ctn = dot(wpk, ct)
    nh, nl = split(ctn)
    both = jnp.concatenate([nh, nl], axis=0)

    def chunk(k):
        where = slice(k * CW, (k + 1) * CW)
        p = dot(both, bh_v[:, where], precision=None)
        t = p[:128] + p[128:] + dot(nh, bl_v[:, where], precision=None)
        tb[k, 0] = t[:64]
        tb[k, 1] = t[64:]
        return send(tb.at[k, 1 - core], tc.at[k], tss.at[k], trs.at[k], dev(fc=1))

    def after_core(k):
        t_core[k].wait_recv()
        v = tb[k, core] + tc[k]
        for q in range(NX):
            ts[k, q] = v[16 * q : 16 * (q + 1)]
        return [
            send(ts.at[k, (x + dx) % NX], xr.at[k, dx - 1], xss.at[k, dx - 1], xrs.at[k, dx - 1], dev(dx=dx))
            for dx in (2, 1, 3)
        ]

    t_core, t_x = [chunk(0)], []

    total = ms[...]
    for i, copy in enumerate(m_x):
        copy.wait_recv()
        total = total + ma[i]
    mt[...] = total
    m_z = [
        send(mt, mb.at[i], mss.at[7 + i], mrs.at[7 + i], dev(dz=dz, fz=fz))
        for i, (dz, fz) in enumerate(zz)
    ]

    t_core.append(chunk(1))
    t_x.append(after_core(0))
    t_core.append(chunk(2))
    t_x.append(after_core(1))
    t_core.append(chunk(3))
    t_x.append(after_core(2))
    t_x.append(after_core(3))

    for i, copy in enumerate(r_x):
        copy.wait_recv()
    for dx in range(1, NX):
        r_core.append(send(group(dx), group(dx), rs.at[6 + dx], rr.at[6 + dx], dev(fc=1)))

    cbar_out[...] = dot(wk_v[pl.ds(pl.multiple_of(col * 16, 16), 16), :], ct)
    cn = ctn.T
    ch, cl = split(cn)
    x3_v[...] = jnp.concatenate([ch, cl, ch], axis=1)

    same, other = mt[...], None
    for i, (dz, fz) in enumerate(zz):
        m_z[i].wait_recv()
        if fz:
            other = mb[i] if other is None else other + mb[i]
        else:
            same = same + mb[i]
    mg[y, zh] = same
    mg[y, 1 - zh] = other
    m_y = [
        send(mg.at[y], mg.at[y], mss.at[13 + dy], mrs.at[13 + dy], dev(dy=dy)) for dy in (2, 1, 3)
    ]

    for copy in r_core:
        copy.wait_recv()
    for p in range(8):
        v = jnp.concatenate([rg[4 * p + q] for q in range(4)], axis=0)
        high, low = split(v)
        rh_v[16 * p : 16 * (p + 1), :] = high
        rl_v[16 * p : 16 * (p + 1), :] = low

    def r3(k):
        where = slice(k * CW, (k + 1) * CW)
        return jnp.concatenate([rh_v[:, where], rh_v[:, where], rl_v[:, where]], axis=0)

    landed(bb_c)
    for k in range(CH):
        where = slice(k * CW, (k + 1) * CW)
        bbar_out[:, where] = bbar_v[:, where] - dot(x3_v[...], r3(k), precision=None)

    def over_z(k):
        for copy in t_x[k]:
            copy.wait_recv()
        v = ts[k, x] + xr[k, 0] + xr[k, 1] + xr[k, 2]
        for q in range(NZ):
            zs[k, q] = v[4 * q : 4 * q + 4]
        return [
            send(zs.at[k, (zl + dz) % NZ], zr.at[k, dz - 1], zss.at[k, dz - 1], zrs.at[k, dz - 1], dev(dz=dz))
            for dz in range(1, NZ)
        ]

    t_z = [over_z(0), over_z(1)]

    for copy in m_y:
        copy.wait_recv()
    landed(d_c)
    parts = []
    for q in range(NY):
        for h in range(NH):
            lanes = slice(64 * h, 64 * h + 64)
            parts.append(jnp.concatenate([mg[q, 0][:, lanes], mg[q, 1][:, lanes]], axis=1))
    mt_full = jnp.concatenate(parts, axis=0)
    product = dot(wk_v[...], mt_full, ((1,), (1,)))
    mid = d_v[...] - jnp.where(rows >= cols, product, 0.0)
    z = dot(l_v[...].T, mid)
    q = jnp.where(rows >= cols, z, z.T)
    w8 = w_v[pl.ds(pl.multiple_of(row // 2 * 8, 8), 8), :]
    wq = dot(w8, q)
    a8 = dot(wq, w_v[...], ((1,), (1,)))
    a4 = jnp.where(core == 0, a8[:4], a8[4:])
    row4 = lax.broadcasted_iota(jnp.int32, (4, 128), 0) + row * 4
    col4 = lax.broadcasted_iota(jnp.int32, (4, 128), 1)
    kda = jnp.where(row4 > col4, a4, jnp.where(row4 == col4, 0.5 * a4, 0.0))
    pick = lax.broadcasted_iota(jnp.int32, (128, 16), 0) == (
        lax.broadcasted_iota(jnp.int32, (128, 16), 1) + col * 16
    )
    kda_out[...] = dot(kda, jnp.where(pick, 1.0, 0.0))

    ap = dot(wq, wp_v[...], ((1,), (1,)))
    ah, al = split(ap)
    a3 = jnp.concatenate([ah, al, ah], axis=1)
    landed(rb_c)
    for k in range(CH):
        where = slice(k * CW, (k + 1) * CW)
        corr = dot(a3, r3(k), precision=None)
        rbar_v[:, where] = rbar_v[:, where] - jnp.where(core == 0, corr[:4], corr[4:])

    t_z += [over_z(2), over_z(3)]
    for k in range(CH):
        where = slice(k * CW, (k + 1) * CW)
        acc = zs[k, zl]
        for dz in range(1, NZ):
            t_z[k][dz - 1].wait_recv()
            acc = acc + zr[k, dz - 1]
        rbar_out[:, where] = rbar_v[:, where] - acc
    end()


def store(cbar_v, bbar_v, kda_v, rbar_v, cbar_hbm, bbar_hbm, kda_hbm, rbar_hbm, sem):
    copies = [
        pltpu.make_async_copy(bbar_v.at[pl.ds(64 * k, 64)], bbar_hbm.at[pl.ds(64 * k, 64)], sem.at[3 + k])
        for k in range(8)
    ]
    copies += [
        pltpu.make_async_copy(cbar_v, cbar_hbm, sem.at[0]),
        pltpu.make_async_copy(kda_v, kda_hbm, sem.at[1]),
        pltpu.make_async_copy(rbar_v, rbar_hbm, sem.at[2]),
    ]
    for copy in copies:
        copy.start()
    for copy in copies:
        copy.wait()


SHAPES = ((16, 512), (512, 2048), (4, 16), (4, 2048))


def body(c_panel, cbar_in, factor, dbar_in, r_panel, rbar_in, b_block, bbar_in):
    vmem = pltpu.VMEM
    sem = pltpu.SemaphoreType.DMA
    anywhere = pl.BlockSpec(memory_space=pl.ANY)
    in_vmem = pl.BlockSpec(memory_space=vmem)
    scratch = [
        vmem((128, 128), F32), vmem((128, 128), F32), vmem((2, 16, 512), F32), vmem((4, 2048), F32),
        vmem((512, 2048), F32), vmem((512, 2048), F32), vmem((512, 2048), BF16), vmem((512, 2048), BF16),
        vmem((NH, NY, 16, 512), F32), vmem((32, 4, 2048), F32),
        vmem((128, 128), F32), vmem((128, 128), F32), vmem((128, 128), F32),
        vmem((512, 384), BF16), vmem((128, 2048), BF16), vmem((128, 2048), BF16),
        vmem((CH, 2, 64, CW), F32), vmem((CH, 64, CW), F32), vmem((CH, NX, 16, CW), F32),
        vmem((CH, NX - 1, 16, CW), F32),
        vmem((CH, NZ, 4, CW), F32), vmem((CH, NZ - 1, 4, CW), F32),
        vmem((16, 128), F32), vmem((7, 16, 128), F32), vmem((16, 128), F32), vmem((7, 16, 128), F32),
        vmem((NY, NH, 16, 128), F32),
        sem((7,)), sem((CH,)),
        sem((8,)), sem((8,)), sem((10,)), sem((10,)), sem((CH,)), sem((CH,)),
        sem((CH, 3)), sem((CH, 3)), sem((CH, 3)), sem((CH, 3)), sem((17,)), sem((17,)),
    ]
    args = (c_panel.T, cbar_in.T, factor, dbar_in, r_panel, rbar_in, b_block, bbar_in)
    args = [pltpu.with_memory_space_constraint(a, pltpu.HBM) for a in args]
    results = pl.pallas_call(
        kernel,
        out_shape=[vmem(shape, F32) for shape in SHAPES],
        in_specs=[anywhere] * 8,
        out_specs=[in_vmem] * 4,
        scratch_shapes=scratch,
        compiler_params=pltpu.CompilerParams(
            collective_id=0, has_side_effects=True, vmem_limit_bytes=32 * 1024 * 1024
        ),
        name="block_step",
    )(*args)
    results = [pltpu.with_memory_space_constraint(a, vmem) for a in results]
    cbar_t, bbar_out, kda, rbar_out = pl.pallas_call(
        store,
        out_shape=[jax.ShapeDtypeStruct(shape, F32) for shape in SHAPES],
        in_specs=[anywhere] * 4,
        out_specs=[anywhere] * 4,
        scratch_shapes=[sem((11,))],
        compiler_params=pltpu.CompilerParams(vmem_limit_bytes=4 * 1024 * 1024),
        name="store",
    )(*results)
    return cbar_t.T, bbar_out, kda, rbar_out


def solution(mesh):
    spec = P("row", "col")
    in_specs = (spec, spec, P(), P(), spec, spec, spec, spec)
    return jax.shard_map(
        body, mesh=mesh, in_specs=in_specs, out_specs=(spec,) * 4, check_vma=False
    )
```

```python
import jax
import jax.numpy as jnp
from jax import lax
from jax.experimental import pallas as pl
from jax.experimental.pallas import tpu as pltpu
from jax.sharding import PartitionSpec as P

F32 = jnp.float32
BF16 = jnp.bfloat16
HI = lax.Precision.HIGHEST
MESH = pl.DeviceIdType.MESH
NX, NZ, NY, NC, NH = 4, 4, 4, 2, 2
CH = 4
CW = 512
ZK = 3


def dot(a, b, contract=((1,), (0,)), precision=HI):
    return lax.dot_general(
        a, b, (contract, ((), ())), precision=precision, preferred_element_type=F32
    )


def split(a):
    high = a.astype(BF16)
    return high, (a - high.astype(F32)).astype(BF16)


def kernel(
    c_hbm, cbar_hbm, l_hbm, d_hbm, r_hbm, rbar_hbm, b_hbm, bbar_hbm,
    cbar_out, bbar_out, kda_out, rbar_out,
    l_v, d_v, cc, rbar_v, b_v, bbar_v, bh_v, bl_v,
    cg, rg, w_v, wk_v, wpk_v, uk_v, dk_v, x3_v, rh_v, rl_v,
    tb, tc, ts, xr, zs, zr, z1, zr1, x1, xr1,
    ms, ma, mt, mb, mg,
    lsem, bsem,
    cgs, cgr, rs, rr, tss, trs, xss, xrs, zss, zrs, mss, mrs,
):
    row, col = lax.axis_index("row"), lax.axis_index("col")
    core, x, zl = row % NC, (row // NC) % NX, row // (NC * NX)
    y, zh = col // NH, col % NH

    def dev(dz=0, dx=0, fc=0, dy=0, fz=0):
        c2 = 1 - core if fc else core
        h2 = 1 - zh if fz else zh
        z2, x2, y2 = (zl + dz) % NZ, (x + dx) % NX, (y + dy) % NY
        return (z2 * (NX * NC) + x2 * NC + c2, y2 * NH + h2)

    xc = [(dx, fc) for dx in range(NX) for fc in range(NC)][1:]
    zz = [(dz, fz) for dz in range(NZ) for fz in range(NH)][1:]
    peers = [dev(dz=dz, fz=fz) for dz, fz in reversed(zz)]
    peers += [dev(dy=dy) for dy in (2, 1, 3)]
    peers += [dev(dx=dx, fc=fc) for dx, fc in xc]

    barrier = pltpu.get_barrier_semaphore()
    for peer in peers:
        pl.semaphore_signal(barrier, inc=1, device_id=peer, device_id_type=MESH)

    pending = []

    def local(src, dst, sem):
        copy = pltpu.make_async_copy(src, dst, sem)
        copy.start()
        pending.append(copy)
        return copy

    def landed(copy):
        copy.wait()
        pending[:] = [other for other in pending if other is not copy]

    sent = []

    def send(src, dst, ssem, rsem, to):
        copy = pltpu.make_async_remote_copy(
            src_ref=src, dst_ref=dst, send_sem=ssem, recv_sem=rsem,
            device_id=to, device_id_type=MESH,
        )
        copy.start()
        sent.append(copy)
        return copy

    def end():
        for copy in pending:
            copy.wait()
        for copy in sent:
            copy.wait_send()

    my_slot = core * (NX * NZ) + x * NZ + zl
    l_c = local(l_hbm, l_v, lsem.at[0])
    cg_c = local(cbar_hbm, cg.at[zh, y], lsem.at[1])
    c_c = local(c_hbm, cc.at[y], lsem.at[2])
    r_c = local(r_hbm, rg.at[my_slot], lsem.at[3])
    d_c = local(d_hbm, d_v, lsem.at[4])
    rb_c = local(rbar_hbm, rbar_v, lsem.at[5])
    b_c = [
        local(b_hbm.at[:, pl.ds(k * CW, CW)], b_v.at[:, pl.ds(k * CW, CW)], bsem.at[k])
        for k in range(CH)
    ]
    bb_c = local(bbar_hbm, bbar_v, lsem.at[6])

    pl.semaphore_wait(barrier, len(peers))

    cz = send(cbar_hbm, cg.at[zh, y], cgs.at[0], cgr.at[0], dev(fz=1))
    cy = [
        send(cbar_hbm, cg.at[zh, y], cgs.at[dy], cgr.at[dy], dev(dy=dy)) for dy in (2, 1, 3)
    ]
    cc_y = [send(c_hbm, cc.at[y], cgs.at[6 + dy], cgr.at[6 + dy], dev(dy=dy)) for dy in (2, 1, 3)]
    rz = [
        send(r_hbm, rg.at[my_slot], rs.at[dz - 1], rr.at[dz - 1], dev(dz=dz))
        for dz in range(1, NZ)
    ]
    r_x = [
        send(r_hbm, rg.at[my_slot], rs.at[2 + dx], rr.at[2 + dx], dev(dx=dx)) for dx in (2, 1, 3)
    ]

    rows = lax.broadcasted_iota(jnp.int32, (128, 128), 0)
    cols = lax.broadcasted_iota(jnp.int32, (128, 128), 1)
    landed(l_c)
    u = l_v[...].T
    eye = rows == cols
    w = jnp.where(eye, 1.0 / jnp.where(eye, u, 1.0), 0.0)
    for s in (1, 2, 4, 8, 16, 32, 64):
        mask = (rows // (2 * s) == cols // (2 * s)) & (rows % (2 * s) < s) & (cols % (2 * s) >= s)
        w = w - dot(dot(w, jnp.where(mask, u, 0.0)), w)
    w_v[...] = w
    order_c = ((cols % 64) // 16 * 2 + cols // 64) * 16 + cols % 16
    wk = dot(w, jnp.where(rows == order_c, 1.0, 0.0))
    wk_v[...] = wk
    order_r = ((rows % 64) // 16 * 2 + rows // 64) * 16 + rows % 16
    uk_v[...] = dot(jnp.where(cols == order_r, 1.0, 0.0), u)
    landed(d_c)
    dk_v[...] = dot(d_v[...], jnp.where(rows == order_c, 1.0, 0.0))
    natural = (rows % 16) // 4 * 32 + (rows // 16) % 4 * 8 + rows // 64 * 4 + rows % 4
    order = jnp.where(cols == natural, 1.0, 0.0)
    wpk = dot(order, wk)
    wpk_v[...] = wpk

    for k in range(CH):
        landed(b_c[k])
        high, low = split(b_v[:, k * CW : (k + 1) * CW])
        bh_v[:, k * CW : (k + 1) * CW] = high
        bl_v[:, k * CW : (k + 1) * CW] = low

    cz.wait_recv()
    part = cg.at[1 - zh, y]
    cy2 = [send(part, part, cgs.at[3 + dy], cgr.at[3 + dy], dev(dy=dy)) for dy in (2, 1, 3)]

    for copy in cc_y:
        copy.wait_recv()
    landed(cg_c)
    landed(c_c)
    pt = dot(jnp.concatenate([cg[0, y], cg[1, y]], axis=0), cc[...].reshape(64, 512), ((1,), (1,)))
    ms[...] = jnp.concatenate([pt[:16], pt[16:]], axis=1)
    m_x = [
        send(ms, ma.at[i], mss.at[i], mrs.at[i], dev(dx=dx, fc=fc))
        for i, (dx, fc) in enumerate(xc)
    ]

    for copy in rz:
        copy.wait_recv()
    landed(r_c)

    def group(g):
        return rg.at[pl.ds(core * (NX * NZ) + ((x + g) % NX) * NZ, NZ)]

    for dz in range(1, NZ):
        slot = rg.at[core * (NX * NZ) + x * NZ + (zl + dz) % NZ]
        r_x += [
            send(slot, slot, rs.at[3 * dz + 2 + dx], rr.at[3 * dz + 2 + dx], dev(dx=dx))
            for dx in (2, 1, 3)
        ]
    r_core = [send(group(0), group(0), rs.at[15], rr.at[15], dev(fc=1))]

    for copy in cy + cy2:
        copy.wait_recv()
    ct = cg[...].reshape(128, 512)
    ctn = dot(wpk, ct)
    nh, nl = split(ctn)
    both = jnp.concatenate([nh, nl], axis=0)

    def chunk(k):
        where = slice(k * CW, (k + 1) * CW)
        p = dot(both, bh_v[:, where], precision=None)
        t = p[:128] + p[128:] + dot(nh, bl_v[:, where], precision=None)
        tb[k, 0] = t[:64]
        tb[k, 1] = t[64:]
        return send(tb.at[k, 1 - core], tc.at[k], tss.at[k], trs.at[k], dev(fc=1))

    def after_core(k):
        t_core[k].wait_recv()
        v = tb[k, core] + tc[k]
        if k == ZK:
            for q in range(NX):
                for p in range(NZ):
                    z1[p, q] = v[16 * q + 4 * p : 16 * q + 4 * p + 4]
            return [
                send(z1.at[(zl + dz) % NZ], zr1.at[dz - 1], zss.at[k, dz - 1], zrs.at[k, dz - 1], dev(dz=dz))
                for dz in range(1, NZ)
            ]
        for q in range(NX):
            ts[k, q] = v[16 * q : 16 * (q + 1)]
        return [
            send(ts.at[k, (x + dx) % NX], xr.at[k, dx - 1], xss.at[k, dx - 1], xrs.at[k, dx - 1], dev(dx=dx))
            for dx in (2, 1, 3)
        ]

    t_core = [chunk(k) for k in range(CH)]
    t_1 = [after_core(0)]

    total = ms[...]
    for i, copy in enumerate(m_x):
        copy.wait_recv()
        total = total + ma[i]
    mt[...] = total
    m_z = [
        send(mt, mb.at[i], mss.at[7 + i], mrs.at[7 + i], dev(dz=dz, fz=fz))
        for i, (dz, fz) in enumerate(zz)
    ]
    t_1 += [after_core(k) for k in range(1, CH)]

    for copy in r_x:
        copy.wait_recv()
    for dx in range(1, NX):
        r_core.append(send(group(dx), group(dx), rs.at[15 + dx], rr.at[15 + dx], dev(fc=1)))

    cbar_out[...] = dot(wk_v[pl.ds(pl.multiple_of(col * 16, 16), 16), :], ct)
    cn = ctn.T
    ch, cl = split(cn)
    x3_v[...] = jnp.concatenate([ch, cl, ch], axis=1)

    same, other = mt[...], None
    for i, (dz, fz) in enumerate(zz):
        m_z[i].wait_recv()
        if fz:
            other = mb[i] if other is None else other + mb[i]
        else:
            same = same + mb[i]
    mg[y, zh] = same
    mg[y, 1 - zh] = other
    m_y = [
        send(mg.at[y], mg.at[y], mss.at[13 + dy], mrs.at[13 + dy], dev(dy=dy)) for dy in (2, 1, 3)
    ]

    for copy in r_core:
        copy.wait_recv()
    for p in range(8):
        v = jnp.concatenate([rg[4 * p + q] for q in range(4)], axis=0)
        high, low = split(v)
        rh_v[16 * p : 16 * (p + 1), :] = high
        rl_v[16 * p : 16 * (p + 1), :] = low

    def r3(k):
        where = slice(k * CW, (k + 1) * CW)
        return jnp.concatenate([rh_v[:, where], rh_v[:, where], rl_v[:, where]], axis=0)

    landed(bb_c)
    for k in range(CH):
        where = slice(k * CW, (k + 1) * CW)
        bbar_out[:, where] = bbar_v[:, where] - dot(x3_v[...], r3(k), precision=None)

    def second_axis(k):
        for copy in t_1[k]:
            copy.wait_recv()
        if k == ZK:
            x1[...] = z1[zl] + zr1[0] + zr1[1] + zr1[2]
            return [
                send(x1.at[(x + dx) % NX], xr1.at[dx - 1], xss.at[k, dx - 1], xrs.at[k, dx - 1], dev(dx=dx))
                for dx in (2, 1, 3)
            ]
        v = ts[k, x] + xr[k, 0] + xr[k, 1] + xr[k, 2]
        for q in range(NZ):
            zs[k, q] = v[4 * q : 4 * q + 4]
        return [
            send(zs.at[k, (zl + dz) % NZ], zr.at[k, dz - 1], zss.at[k, dz - 1], zrs.at[k, dz - 1], dev(dz=dz))
            for dz in range(1, NZ)
        ]

    t_2 = {k: second_axis(k) for k in (0, 1, ZK, 2)}

    for copy in m_y:
        copy.wait_recv()
    parts = []
    for q in range(NY):
        for h in range(NH):
            lanes = slice(64 * h, 64 * h + 64)
            parts.append(jnp.concatenate([mg[q, 0][:, lanes], mg[q, 1][:, lanes]], axis=1))
    mt_full = jnp.concatenate(parts, axis=0)
    mid = dk_v[...] - jnp.where(rows >= order_c, dot(w_v[...], mt_full), 0.0)
    z = dot(uk_v[...], mid)
    q = jnp.where(order_r >= order_c, z, z.T)
    w8 = wk_v[pl.ds(pl.multiple_of(row // 2 * 8, 8), 8), :]
    wq = dot(w8, q)
    a8 = dot(wq, wk_v[...], ((1,), (1,)))
    a4 = jnp.where(core == 0, a8[:4], a8[4:])
    row4 = lax.broadcasted_iota(jnp.int32, (4, 128), 0) + row * 4
    col4 = lax.broadcasted_iota(jnp.int32, (4, 128), 1)
    kda = jnp.where(row4 > col4, a4, jnp.where(row4 == col4, 0.5 * a4, 0.0))
    pick = lax.broadcasted_iota(jnp.int32, (128, 16), 0) == (
        lax.broadcasted_iota(jnp.int32, (128, 16), 1) + col * 16
    )
    kda_out[...] = dot(kda, jnp.where(pick, 1.0, 0.0))

    ap = dot(wq, wpk_v[...], ((1,), (1,)))
    ah, al = split(ap)
    a3 = jnp.concatenate([ah, al, ah], axis=1)
    landed(rb_c)
    for k in range(CH):
        where = slice(k * CW, (k + 1) * CW)
        corr = dot(a3, r3(k), precision=None)
        rbar_v[:, where] = rbar_v[:, where] - jnp.where(core == 0, corr[:4], corr[4:])
    for k in range(CH):
        where = slice(k * CW, (k + 1) * CW)
        for copy in t_2[k]:
            copy.wait_recv()
        if k == ZK:
            acc = x1[x] + xr1[0] + xr1[1] + xr1[2]
        else:
            acc = zs[k, zl] + zr[k, 0] + zr[k, 1] + zr[k, 2]
        rbar_out[:, where] = rbar_v[:, where] - acc
    end()


def store(cbar_v, bbar_v, kda_v, rbar_v, cbar_hbm, bbar_hbm, kda_hbm, rbar_hbm, sem):
    copies = [
        pltpu.make_async_copy(bbar_v.at[pl.ds(64 * k, 64)], bbar_hbm.at[pl.ds(64 * k, 64)], sem.at[3 + k])
        for k in range(8)
    ]
    copies += [
        pltpu.make_async_copy(cbar_v, cbar_hbm, sem.at[0]),
        pltpu.make_async_copy(kda_v, kda_hbm, sem.at[1]),
        pltpu.make_async_copy(rbar_v, rbar_hbm, sem.at[2]),
    ]
    for copy in copies:
        copy.start()
    for copy in copies:
        copy.wait()


SHAPES = ((16, 512), (512, 2048), (4, 16), (4, 2048))


def body(c_panel, cbar_in, factor, dbar_in, r_panel, rbar_in, b_block, bbar_in):
    vmem = pltpu.VMEM
    sem = pltpu.SemaphoreType.DMA
    anywhere = pl.BlockSpec(memory_space=pl.ANY)
    in_vmem = pl.BlockSpec(memory_space=vmem)
    scratch = [
        vmem((128, 128), F32), vmem((128, 128), F32), vmem((NY, 16, 512), F32), vmem((4, 2048), F32),
        vmem((512, 2048), F32), vmem((512, 2048), F32), vmem((512, 2048), BF16), vmem((512, 2048), BF16),
        vmem((NH, NY, 16, 512), F32), vmem((32, 4, 2048), F32),
        vmem((128, 128), F32), vmem((128, 128), F32), vmem((128, 128), F32),
        vmem((128, 128), F32), vmem((128, 128), F32),
        vmem((512, 384), BF16), vmem((128, 2048), BF16), vmem((128, 2048), BF16),
        vmem((CH, 2, 64, CW), F32), vmem((CH, 64, CW), F32), vmem((CH, NX, 16, CW), F32),
        vmem((CH, NX - 1, 16, CW), F32),
        vmem((CH, NZ, 4, CW), F32), vmem((CH, NZ - 1, 4, CW), F32),
        vmem((NZ, NX, 4, CW), F32), vmem((NZ - 1, NX, 4, CW), F32),
        vmem((NX, 4, CW), F32), vmem((NX - 1, 4, CW), F32),
        vmem((16, 128), F32), vmem((7, 16, 128), F32), vmem((16, 128), F32), vmem((7, 16, 128), F32),
        vmem((NY, NH, 16, 128), F32),
        sem((7,)), sem((CH,)),
        sem((10,)), sem((10,)), sem((19,)), sem((19,)), sem((CH,)), sem((CH,)),
        sem((CH, 3)), sem((CH, 3)), sem((CH, 3)), sem((CH, 3)), sem((17,)), sem((17,)),
    ]
    args = (c_panel.T, cbar_in.T, factor, dbar_in, r_panel, rbar_in, b_block, bbar_in)
    args = [pltpu.with_memory_space_constraint(a, pltpu.HBM) for a in args]
    results = pl.pallas_call(
        kernel,
        out_shape=[vmem(shape, F32) for shape in SHAPES],
        in_specs=[anywhere] * 8,
        out_specs=[in_vmem] * 4,
        scratch_shapes=scratch,
        compiler_params=pltpu.CompilerParams(
            collective_id=0, has_side_effects=True, vmem_limit_bytes=32 * 1024 * 1024
        ),
        name="block_step",
    )(*args)
    results = [pltpu.with_memory_space_constraint(a, vmem) for a in results]
    cbar_t, bbar_out, kda, rbar_out = pl.pallas_call(
        store,
        out_shape=[jax.ShapeDtypeStruct(shape, F32) for shape in SHAPES],
        in_specs=[anywhere] * 4,
        out_specs=[anywhere] * 4,
        scratch_shapes=[sem((11,))],
        compiler_params=pltpu.CompilerParams(vmem_limit_bytes=4 * 1024 * 1024),
        name="store",
    )(*results)
    return cbar_t.T, bbar_out, kda, rbar_out


def solution(mesh):
    spec = P("row", "col")
    in_specs = (spec, spec, P(), P(), spec, spec, spec, spec)
    return jax.shard_map(
        body, mesh=mesh, in_specs=in_specs, out_specs=(spec,) * 4, check_vma=False
    )
```

```python
import jax
import jax.numpy as jnp
from jax import lax
from jax.experimental import pallas as pl
from jax.experimental.pallas import tpu as pltpu
from jax.sharding import PartitionSpec as P

F32 = jnp.float32
BF16 = jnp.bfloat16
HI = lax.Precision.HIGHEST
MESH = pl.DeviceIdType.MESH
NX, NZ, NY, NC, NH = 4, 4, 4, 2, 2
CH = 4
CW = 512
ZK = 3


def dot(a, b, contract=((1,), (0,)), precision=HI):
    return lax.dot_general(
        a, b, (contract, ((), ())), precision=precision, preferred_element_type=F32
    )


def split(a):
    high = a.astype(BF16)
    return high, (a - high.astype(F32)).astype(BF16)


def kernel(
    c_hbm, cbar_hbm, l_hbm, d_hbm, r_hbm, rbar_hbm, b_hbm, bbar_hbm,
    cbar_out, bbar_out, kda_out, rbar_out,
    l_v, d_v, cc, rbar_v, b_v, bbar_v, bh_v, bl_v,
    cg, rg, w_v, wk_v, wpk_v, uk_v, dk_v, x3_v, rh_v, rl_v,
    tb, tc, ts, xr, zs, zr, z1, zr1, x1, xr1,
    ms, ma, mt, mb, mg,
    lsem, bsem,
    cgs, cgr, rs, rr, tss, trs, xss, xrs, zss, zrs, mss, mrs,
):
    row, col = lax.axis_index("row"), lax.axis_index("col")
    core, x, zl = row % NC, (row // NC) % NX, row // (NC * NX)
    y, zh = col // NH, col % NH

    def dev(dz=0, dx=0, fc=0, dy=0, fz=0):
        c2 = 1 - core if fc else core
        h2 = 1 - zh if fz else zh
        z2, x2, y2 = (zl + dz) % NZ, (x + dx) % NX, (y + dy) % NY
        return (z2 * (NX * NC) + x2 * NC + c2, y2 * NH + h2)

    xc = [(dx, fc) for dx in range(NX) for fc in range(NC)][1:]
    zz = [(dz, fz) for dz in range(NZ) for fz in range(NH)][1:]
    peers = [dev(dz=dz, fz=fz) for dz, fz in reversed(zz)]
    peers += [dev(dy=dy) for dy in (2, 1, 3)]
    peers += [dev(dx=dx, fc=fc) for dx, fc in xc]

    barrier = pltpu.get_barrier_semaphore()
    for peer in peers:
        pl.semaphore_signal(barrier, inc=1, device_id=peer, device_id_type=MESH)

    pending = []

    def local(src, dst, sem):
        copy = pltpu.make_async_copy(src, dst, sem)
        copy.start()
        pending.append(copy)
        return copy

    def landed(copy):
        copy.wait()
        pending[:] = [other for other in pending if other is not copy]

    sent = []

    def send(src, dst, ssem, rsem, to):
        copy = pltpu.make_async_remote_copy(
            src_ref=src, dst_ref=dst, send_sem=ssem, recv_sem=rsem,
            device_id=to, device_id_type=MESH,
        )
        copy.start()
        sent.append(copy)
        return copy

    def end():
        for copy in pending:
            copy.wait()
        for copy in sent:
            copy.wait_send()

    my_slot = core * (NX * NZ) + x * NZ + zl
    l_c = local(l_hbm, l_v, lsem.at[0])
    cg_c = local(cbar_hbm, cg.at[zh, y], lsem.at[1])
    c_c = local(c_hbm, cc.at[y], lsem.at[2])
    r_c = local(r_hbm, rg.at[my_slot], lsem.at[3])
    d_c = local(d_hbm, d_v, lsem.at[4])
    rb_c = local(rbar_hbm, rbar_v, lsem.at[5])
    b_c = [
        local(b_hbm.at[:, pl.ds(k * CW, CW)], b_v.at[:, pl.ds(k * CW, CW)], bsem.at[k])
        for k in range(CH)
    ]
    bb_c = local(bbar_hbm, bbar_v, lsem.at[6])

    pl.semaphore_wait(barrier, len(peers))

    cz = send(cbar_hbm, cg.at[zh, y], cgs.at[0], cgr.at[0], dev(fz=1))
    cy = [
        send(cbar_hbm, cg.at[zh, y], cgs.at[dy], cgr.at[dy], dev(dy=dy)) for dy in (2, 1, 3)
    ]
    cc_y = [send(c_hbm, cc.at[y], cgs.at[6 + dy], cgr.at[6 + dy], dev(dy=dy)) for dy in (2, 1, 3)]
    rz = [
        send(r_hbm, rg.at[my_slot], rs.at[dz - 1], rr.at[dz - 1], dev(dz=dz))
        for dz in range(1, NZ)
    ]
    r_x = [
        send(r_hbm, rg.at[my_slot], rs.at[2 + dx], rr.at[2 + dx], dev(dx=dx)) for dx in (2, 1, 3)
    ]

    rows = lax.broadcasted_iota(jnp.int32, (128, 128), 0)
    cols = lax.broadcasted_iota(jnp.int32, (128, 128), 1)
    landed(l_c)
    u = l_v[...].T
    eye = rows == cols
    w = jnp.where(eye, 1.0 / jnp.where(eye, u, 1.0), 0.0)
    for s in (1, 2, 4, 8, 16, 32, 64):
        mask = (rows // (2 * s) == cols // (2 * s)) & (rows % (2 * s) < s) & (cols % (2 * s) >= s)
        w = w - dot(dot(w, jnp.where(mask, u, 0.0)), w)
    w_v[...] = w


    cz.wait_recv()
    part = cg.at[1 - zh, y]
    cy2 = [send(part, part, cgs.at[3 + dy], cgr.at[3 + dy], dev(dy=dy)) for dy in (2, 1, 3)]

    for copy in cc_y:
        copy.wait_recv()
    landed(cg_c)
    landed(c_c)
    pt = dot(jnp.concatenate([cg[0, y], cg[1, y]], axis=0), cc[...].reshape(64, 512), ((1,), (1,)))
    ms[...] = jnp.concatenate([pt[:16], pt[16:]], axis=1)
    m_x = [
        send(ms, ma.at[i], mss.at[i], mrs.at[i], dev(dx=dx, fc=fc))
        for i, (dx, fc) in enumerate(xc)
    ]

    for copy in rz:
        copy.wait_recv()
    landed(r_c)

    def group(g):
        return rg.at[pl.ds(core * (NX * NZ) + ((x + g) % NX) * NZ, NZ)]

    for dz in range(1, NZ):
        slot = rg.at[core * (NX * NZ) + x * NZ + (zl + dz) % NZ]
        r_x += [
            send(slot, slot, rs.at[3 * dz + 2 + dx], rr.at[3 * dz + 2 + dx], dev(dx=dx))
            for dx in (2, 1, 3)
        ]
    r_core = [send(group(0), group(0), rs.at[15], rr.at[15], dev(fc=1))]
    order_c = ((cols % 64) // 16 * 2 + cols // 64) * 16 + cols % 16
    wk = dot(w, jnp.where(rows == order_c, 1.0, 0.0))
    wk_v[...] = wk
    order_r = ((rows % 64) // 16 * 2 + rows // 64) * 16 + rows % 16
    uk_v[...] = dot(jnp.where(cols == order_r, 1.0, 0.0), u)
    landed(d_c)
    dk_v[...] = dot(d_v[...], jnp.where(rows == order_c, 1.0, 0.0))
    natural = (rows % 16) // 4 * 32 + (rows // 16) % 4 * 8 + rows // 64 * 4 + rows % 4
    order = jnp.where(cols == natural, 1.0, 0.0)
    wpk = dot(order, wk)
    wpk_v[...] = wpk

    for k in range(CH):
        landed(b_c[k])
        high, low = split(b_v[:, k * CW : (k + 1) * CW])
        bh_v[:, k * CW : (k + 1) * CW] = high
        bl_v[:, k * CW : (k + 1) * CW] = low

    for copy in cy + cy2:
        copy.wait_recv()
    ct = cg[...].reshape(128, 512)
    ctn = dot(wpk, ct)
    nh, nl = split(ctn)
    both = jnp.concatenate([nh, nl], axis=0)

    def chunk(k):
        where = slice(k * CW, (k + 1) * CW)
        p = dot(both, bh_v[:, where], precision=None)
        t = p[:128] + p[128:] + dot(nh, bl_v[:, where], precision=None)
        tb[k, 0] = t[:64]
        tb[k, 1] = t[64:]
        return send(tb.at[k, 1 - core], tc.at[k], tss.at[k], trs.at[k], dev(fc=1))

    def after_core(k):
        t_core[k].wait_recv()
        v = tb[k, core] + tc[k]
        if k == ZK:
            for q in range(NX):
                for p in range(NZ):
                    z1[p, q] = v[16 * q + 4 * p : 16 * q + 4 * p + 4]
            return [
                send(z1.at[(zl + dz) % NZ], zr1.at[dz - 1], zss.at[k, dz - 1], zrs.at[k, dz - 1], dev(dz=dz))
                for dz in range(1, NZ)
            ]
        for q in range(NX):
            ts[k, q] = v[16 * q : 16 * (q + 1)]
        return [
            send(ts.at[k, (x + dx) % NX], xr.at[k, dx - 1], xss.at[k, dx - 1], xrs.at[k, dx - 1], dev(dx=dx))
            for dx in (2, 1, 3)
        ]

    t_core = [chunk(k) for k in range(CH)]

    total = ms[...]
    for i, copy in enumerate(m_x):
        copy.wait_recv()
        total = total + ma[i]
    mt[...] = total
    m_z = [
        send(mt, mb.at[i], mss.at[7 + i], mrs.at[7 + i], dev(dz=dz, fz=fz))
        for i, (dz, fz) in enumerate(zz)
    ]
    t_1 = [after_core(k) for k in range(CH)]

    for copy in r_x:
        copy.wait_recv()
    for dx in range(1, NX):
        r_core.append(send(group(dx), group(dx), rs.at[15 + dx], rr.at[15 + dx], dev(fc=1)))

    cbar_out[...] = dot(wk_v[pl.ds(pl.multiple_of(col * 16, 16), 16), :], ct)
    cn = ctn.T
    ch, cl = split(cn)
    x3_v[...] = jnp.concatenate([ch, cl, ch], axis=1)

    same, other = mt[...], None
    for i, (dz, fz) in enumerate(zz):
        m_z[i].wait_recv()
        if fz:
            other = mb[i] if other is None else other + mb[i]
        else:
            same = same + mb[i]
    mg[y, zh] = same
    mg[y, 1 - zh] = other
    m_y = [
        send(mg.at[y], mg.at[y], mss.at[13 + dy], mrs.at[13 + dy], dev(dy=dy)) for dy in (2, 1, 3)
    ]

    for copy in r_core:
        copy.wait_recv()
    for p in range(8):
        v = jnp.concatenate([rg[4 * p + q] for q in range(4)], axis=0)
        high, low = split(v)
        rh_v[16 * p : 16 * (p + 1), :] = high
        rl_v[16 * p : 16 * (p + 1), :] = low

    def r3(k):
        where = slice(k * CW, (k + 1) * CW)
        return jnp.concatenate([rh_v[:, where], rh_v[:, where], rl_v[:, where]], axis=0)

    landed(bb_c)
    for k in range(CH):
        where = slice(k * CW, (k + 1) * CW)
        bbar_out[:, where] = bbar_v[:, where] - dot(x3_v[...], r3(k), precision=None)

    def second_axis(k):
        for copy in t_1[k]:
            copy.wait_recv()
        if k == ZK:
            x1[...] = z1[zl] + zr1[0] + zr1[1] + zr1[2]
            return [
                send(x1.at[(x + dx) % NX], xr1.at[dx - 1], xss.at[k, dx - 1], xrs.at[k, dx - 1], dev(dx=dx))
                for dx in (2, 1, 3)
            ]
        v = ts[k, x] + xr[k, 0] + xr[k, 1] + xr[k, 2]
        for q in range(NZ):
            zs[k, q] = v[4 * q : 4 * q + 4]
        return [
            send(zs.at[k, (zl + dz) % NZ], zr.at[k, dz - 1], zss.at[k, dz - 1], zrs.at[k, dz - 1], dev(dz=dz))
            for dz in range(1, NZ)
        ]

    t_2 = {k: second_axis(k) for k in (0, 1, ZK, 2)}

    for copy in m_y:
        copy.wait_recv()
    parts = []
    for q in range(NY):
        for h in range(NH):
            lanes = slice(64 * h, 64 * h + 64)
            parts.append(jnp.concatenate([mg[q, 0][:, lanes], mg[q, 1][:, lanes]], axis=1))
    mt_full = jnp.concatenate(parts, axis=0)
    mid = dk_v[...] - jnp.where(rows >= order_c, dot(w_v[...], mt_full), 0.0)
    z = dot(uk_v[...], mid)
    q = jnp.where(order_r >= order_c, z, z.T)
    w8 = wk_v[pl.ds(pl.multiple_of(row // 2 * 8, 8), 8), :]
    wq = dot(w8, q)
    a8 = dot(wq, wk_v[...], ((1,), (1,)))
    a4 = jnp.where(core == 0, a8[:4], a8[4:])
    row4 = lax.broadcasted_iota(jnp.int32, (4, 128), 0) + row * 4
    col4 = lax.broadcasted_iota(jnp.int32, (4, 128), 1)
    kda = jnp.where(row4 > col4, a4, jnp.where(row4 == col4, 0.5 * a4, 0.0))
    pick = lax.broadcasted_iota(jnp.int32, (128, 16), 0) == (
        lax.broadcasted_iota(jnp.int32, (128, 16), 1) + col * 16
    )
    kda_out[...] = dot(kda, jnp.where(pick, 1.0, 0.0))

    ap = dot(wq, wpk_v[...], ((1,), (1,)))
    ah, al = split(ap)
    a3 = jnp.concatenate([ah, al, ah], axis=1)
    landed(rb_c)
    for k in range(CH):
        where = slice(k * CW, (k + 1) * CW)
        corr = dot(a3, r3(k), precision=None)
        rbar_v[:, where] = rbar_v[:, where] - jnp.where(core == 0, corr[:4], corr[4:])
    for k in range(CH):
        where = slice(k * CW, (k + 1) * CW)
        for copy in t_2[k]:
            copy.wait_recv()
        if k == ZK:
            acc = x1[x] + xr1[0] + xr1[1] + xr1[2]
        else:
            acc = zs[k, zl] + zr[k, 0] + zr[k, 1] + zr[k, 2]
        rbar_out[:, where] = rbar_v[:, where] - acc
    end()


def store(cbar_v, bbar_v, kda_v, rbar_v, cbar_hbm, bbar_hbm, kda_hbm, rbar_hbm, sem):
    copies = [
        pltpu.make_async_copy(bbar_v.at[pl.ds(64 * k, 64)], bbar_hbm.at[pl.ds(64 * k, 64)], sem.at[3 + k])
        for k in range(8)
    ]
    copies += [
        pltpu.make_async_copy(cbar_v, cbar_hbm, sem.at[0]),
        pltpu.make_async_copy(kda_v, kda_hbm, sem.at[1]),
        pltpu.make_async_copy(rbar_v, rbar_hbm, sem.at[2]),
    ]
    for copy in copies:
        copy.start()
    for copy in copies:
        copy.wait()


SHAPES = ((16, 512), (512, 2048), (4, 16), (4, 2048))


def body(c_panel, cbar_in, factor, dbar_in, r_panel, rbar_in, b_block, bbar_in):
    vmem = pltpu.VMEM
    sem = pltpu.SemaphoreType.DMA
    anywhere = pl.BlockSpec(memory_space=pl.ANY)
    in_vmem = pl.BlockSpec(memory_space=vmem)
    scratch = [
        vmem((128, 128), F32), vmem((128, 128), F32), vmem((NY, 16, 512), F32), vmem((4, 2048), F32),
        vmem((512, 2048), F32), vmem((512, 2048), F32), vmem((512, 2048), BF16), vmem((512, 2048), BF16),
        vmem((NH, NY, 16, 512), F32), vmem((32, 4, 2048), F32),
        vmem((128, 128), F32), vmem((128, 128), F32), vmem((128, 128), F32),
        vmem((128, 128), F32), vmem((128, 128), F32),
        vmem((512, 384), BF16), vmem((128, 2048), BF16), vmem((128, 2048), BF16),
        vmem((CH, 2, 64, CW), F32), vmem((CH, 64, CW), F32), vmem((CH, NX, 16, CW), F32),
        vmem((CH, NX - 1, 16, CW), F32),
        vmem((CH, NZ, 4, CW), F32), vmem((CH, NZ - 1, 4, CW), F32),
        vmem((NZ, NX, 4, CW), F32), vmem((NZ - 1, NX, 4, CW), F32),
        vmem((NX, 4, CW), F32), vmem((NX - 1, 4, CW), F32),
        vmem((16, 128), F32), vmem((7, 16, 128), F32), vmem((16, 128), F32), vmem((7, 16, 128), F32),
        vmem((NY, NH, 16, 128), F32),
        sem((7,)), sem((CH,)),
        sem((10,)), sem((10,)), sem((19,)), sem((19,)), sem((CH,)), sem((CH,)),
        sem((CH, 3)), sem((CH, 3)), sem((CH, 3)), sem((CH, 3)), sem((17,)), sem((17,)),
    ]
    args = (c_panel.T, cbar_in.T, factor, dbar_in, r_panel, rbar_in, b_block, bbar_in)
    args = [pltpu.with_memory_space_constraint(a, pltpu.HBM) for a in args]
    results = pl.pallas_call(
        kernel,
        out_shape=[vmem(shape, F32) for shape in SHAPES],
        in_specs=[anywhere] * 8,
        out_specs=[in_vmem] * 4,
        scratch_shapes=scratch,
        compiler_params=pltpu.CompilerParams(
            collective_id=0, has_side_effects=True, vmem_limit_bytes=32 * 1024 * 1024
        ),
        name="block_step",
    )(*args)
    results = [pltpu.with_memory_space_constraint(a, vmem) for a in results]
    cbar_t, bbar_out, kda, rbar_out = pl.pallas_call(
        store,
        out_shape=[jax.ShapeDtypeStruct(shape, F32) for shape in SHAPES],
        in_specs=[anywhere] * 4,
        out_specs=[anywhere] * 4,
        scratch_shapes=[sem((11,))],
        compiler_params=pltpu.CompilerParams(vmem_limit_bytes=4 * 1024 * 1024),
        name="store",
    )(*results)
    return cbar_t.T, bbar_out, kda, rbar_out


def solution(mesh):
    spec = P("row", "col")
    in_specs = (spec, spec, P(), P(), spec, spec, spec, spec)
    return jax.shard_map(
        body, mesh=mesh, in_specs=in_specs, out_specs=(spec,) * 4, check_vma=False
    )
```

```python
import jax
import jax.numpy as jnp
from jax import lax
from jax.experimental import pallas as pl
from jax.experimental.pallas import tpu as pltpu
from jax.sharding import PartitionSpec as P

F32 = jnp.float32
BF16 = jnp.bfloat16
HI = lax.Precision.HIGHEST
MESH = pl.DeviceIdType.MESH
NX, NZ, NY, NC, NH = 4, 4, 4, 2, 2
CH = 4
CW = 512
CUTS = (0, 512, 1536, 2048)
NK = 3
ZK = 2


def dot(a, b, contract=((1,), (0,)), precision=HI):
    return lax.dot_general(
        a, b, (contract, ((), ())), precision=precision, preferred_element_type=F32
    )


def split(a):
    high = a.astype(BF16)
    return high, (a - high.astype(F32)).astype(BF16)


def kernel(
    c_hbm, cbar_hbm, l_hbm, d_hbm, r_hbm, rbar_hbm, b_hbm, bbar_hbm,
    cbar_out, bbar_out, kda_out, rbar_out,
    l_v, d_v, cc, rbar_v, b_v, bbar_v, bh_v, bl_v,
    cg, rg, w_v, wk_v, wpk_v, uk_v, dk_v, x3_v, rh_v, rl_v,
    tb, tc, ts, xr, zs, zr, z1, zr1, x1, xr1,
    ms, ma, mt, mb, mg,
    lsem, bsem,
    cgs, cgr, rs, rr, tss, trs, xss, xrs, zss, zrs, mss, mrs,
):
    row, col = lax.axis_index("row"), lax.axis_index("col")
    core, x, zl = row % NC, (row // NC) % NX, row // (NC * NX)
    y, zh = col // NH, col % NH

    def dev(dz=0, dx=0, fc=0, dy=0, fz=0):
        c2 = 1 - core if fc else core
        h2 = 1 - zh if fz else zh
        z2, x2, y2 = (zl + dz) % NZ, (x + dx) % NX, (y + dy) % NY
        return (z2 * (NX * NC) + x2 * NC + c2, y2 * NH + h2)

    xc = [(dx, fc) for dx in range(NX) for fc in range(NC)][1:]
    zz = [(dz, fz) for dz in range(NZ) for fz in range(NH)][1:]
    peers = [dev(dz=dz, fz=fz) for dz, fz in reversed(zz)]
    peers += [dev(dy=dy) for dy in (2, 1, 3)]
    peers += [dev(dx=dx, fc=fc) for dx, fc in xc]

    barrier = pltpu.get_barrier_semaphore()
    for peer in peers:
        pl.semaphore_signal(barrier, inc=1, device_id=peer, device_id_type=MESH)

    pending = []

    def local(src, dst, sem):
        copy = pltpu.make_async_copy(src, dst, sem)
        copy.start()
        pending.append(copy)
        return copy

    def landed(copy):
        copy.wait()
        pending[:] = [other for other in pending if other is not copy]

    sent = []

    def send(src, dst, ssem, rsem, to):
        copy = pltpu.make_async_remote_copy(
            src_ref=src, dst_ref=dst, send_sem=ssem, recv_sem=rsem,
            device_id=to, device_id_type=MESH,
        )
        copy.start()
        sent.append(copy)
        return copy

    def end():
        for copy in pending:
            copy.wait()
        for copy in sent:
            copy.wait_send()

    my_slot = core * (NX * NZ) + x * NZ + zl
    l_c = local(l_hbm, l_v, lsem.at[0])
    cg_c = local(cbar_hbm, cg.at[zh, y], lsem.at[1])
    c_c = local(c_hbm, cc.at[y], lsem.at[2])
    r_c = local(r_hbm, rg.at[my_slot], lsem.at[3])
    d_c = local(d_hbm, d_v, lsem.at[4])
    rb_c = local(rbar_hbm, rbar_v, lsem.at[5])
    b_c = [
        local(b_hbm.at[:, pl.ds(k * CW, CW)], b_v.at[:, pl.ds(k * CW, CW)], bsem.at[k])
        for k in range(CH)
    ]
    bb_c = local(bbar_hbm, bbar_v, lsem.at[6])

    pl.semaphore_wait(barrier, len(peers))

    cz = send(cbar_hbm, cg.at[zh, y], cgs.at[0], cgr.at[0], dev(fz=1))
    cy = [
        send(cbar_hbm, cg.at[zh, y], cgs.at[dy], cgr.at[dy], dev(dy=dy)) for dy in (2, 1, 3)
    ]
    cc_y = [send(c_hbm, cc.at[y], cgs.at[6 + dy], cgr.at[6 + dy], dev(dy=dy)) for dy in (2, 1, 3)]
    rz = [
        send(r_hbm, rg.at[my_slot], rs.at[dz - 1], rr.at[dz - 1], dev(dz=dz))
        for dz in range(1, NZ)
    ]
    r_x = [
        send(r_hbm, rg.at[my_slot], rs.at[2 + dx], rr.at[2 + dx], dev(dx=dx)) for dx in (2, 1, 3)
    ]

    rows = lax.broadcasted_iota(jnp.int32, (128, 128), 0)
    cols = lax.broadcasted_iota(jnp.int32, (128, 128), 1)
    landed(l_c)
    u = l_v[...].T
    eye = rows == cols
    w = jnp.where(eye, 1.0 / jnp.where(eye, u, 1.0), 0.0)
    for s in (1, 2, 4, 8, 16, 32, 64):
        mask = (rows // (2 * s) == cols // (2 * s)) & (rows % (2 * s) < s) & (cols % (2 * s) >= s)
        w = w - dot(dot(w, jnp.where(mask, u, 0.0)), w)
    w_v[...] = w


    cz.wait_recv()
    part = cg.at[1 - zh, y]
    cy2 = [send(part, part, cgs.at[3 + dy], cgr.at[3 + dy], dev(dy=dy)) for dy in (2, 1, 3)]

    for copy in cc_y:
        copy.wait_recv()
    landed(cg_c)
    landed(c_c)
    pt = dot(jnp.concatenate([cg[0, y], cg[1, y]], axis=0), cc[...].reshape(64, 512), ((1,), (1,)))
    ms[...] = jnp.concatenate([pt[:16], pt[16:]], axis=1)
    m_x = [
        send(ms, ma.at[i], mss.at[i], mrs.at[i], dev(dx=dx, fc=fc))
        for i, (dx, fc) in enumerate(xc)
    ]

    for copy in rz:
        copy.wait_recv()
    landed(r_c)

    def group(g):
        return rg.at[pl.ds(core * (NX * NZ) + ((x + g) % NX) * NZ, NZ)]

    for dz in range(1, NZ):
        slot = rg.at[core * (NX * NZ) + x * NZ + (zl + dz) % NZ]
        r_x += [
            send(slot, slot, rs.at[3 * dz + 2 + dx], rr.at[3 * dz + 2 + dx], dev(dx=dx))
            for dx in (2, 1, 3)
        ]
    r_core = [send(group(0), group(0), rs.at[15], rr.at[15], dev(fc=1))]
    order_c = ((cols % 64) // 16 * 2 + cols // 64) * 16 + cols % 16
    wk = dot(w, jnp.where(rows == order_c, 1.0, 0.0))
    wk_v[...] = wk
    order_r = ((rows % 64) // 16 * 2 + rows // 64) * 16 + rows % 16
    uk_v[...] = dot(jnp.where(cols == order_r, 1.0, 0.0), u)
    landed(d_c)
    dk_v[...] = dot(d_v[...], jnp.where(rows == order_c, 1.0, 0.0))
    natural = (rows % 16) // 4 * 32 + (rows // 16) % 4 * 8 + rows // 64 * 4 + rows % 4
    order = jnp.where(cols == natural, 1.0, 0.0)
    wpk = dot(order, wk)
    wpk_v[...] = wpk

    for k in range(CH):
        landed(b_c[k])
        high, low = split(b_v[:, k * CW : (k + 1) * CW])
        bh_v[:, k * CW : (k + 1) * CW] = high
        bl_v[:, k * CW : (k + 1) * CW] = low

    for copy in cy + cy2:
        copy.wait_recv()
    ct = cg[...].reshape(128, 512)
    ctn = dot(wpk, ct)
    nh, nl = split(ctn)
    both = jnp.concatenate([nh, nl], axis=0)

    def chunk(k):
        where, n = slice(CUTS[k], CUTS[k + 1]), CUTS[k + 1] - CUTS[k]
        p = dot(both, bh_v[:, where], precision=None)
        t = p[:128] + p[128:] + dot(nh, bl_v[:, where], precision=None)
        tb[k, 0, :, :n] = t[:64]
        tb[k, 1, :, :n] = t[64:]
        w = pl.ds(0, n)
        return send(tb.at[k, 1 - core, :, w], tc.at[k, :, w], tss.at[k], trs.at[k], dev(fc=1))

    def after_core(k):
        t_core[k].wait_recv()
        n = CUTS[k + 1] - CUTS[k]
        w = pl.ds(0, n)
        v = tb[k, core, :, :n] + tc[k, :, :n]
        if k == ZK:
            for q in range(NX):
                for p in range(NZ):
                    z1[p, q] = v[16 * q + 4 * p : 16 * q + 4 * p + 4]
            return [
                send(z1.at[(zl + dz) % NZ], zr1.at[dz - 1], zss.at[k, dz - 1], zrs.at[k, dz - 1], dev(dz=dz))
                for dz in range(1, NZ)
            ]
        for q in range(NX):
            ts[k, q, :, :n] = v[16 * q : 16 * (q + 1)]
        return [
            send(
                ts.at[k, (x + dx) % NX, :, w], xr.at[k, dx - 1, :, w],
                xss.at[k, dx - 1], xrs.at[k, dx - 1], dev(dx=dx),
            )
            for dx in (2, 1, 3)
        ]

    t_core = [chunk(k) for k in range(NK)]

    total = ms[...]
    for i, copy in enumerate(m_x):
        copy.wait_recv()
        total = total + ma[i]
    mt[...] = total
    m_z = [
        send(mt, mb.at[i], mss.at[7 + i], mrs.at[7 + i], dev(dz=dz, fz=fz))
        for i, (dz, fz) in enumerate(zz)
    ]
    t_1 = [after_core(k) for k in range(NK)]

    for copy in r_x:
        copy.wait_recv()
    for dx in range(1, NX):
        r_core.append(send(group(dx), group(dx), rs.at[15 + dx], rr.at[15 + dx], dev(fc=1)))

    cbar_out[...] = dot(wk_v[pl.ds(pl.multiple_of(col * 16, 16), 16), :], ct)
    cn = ctn.T
    ch, cl = split(cn)
    x3_v[...] = jnp.concatenate([ch, cl, ch], axis=1)

    same, other = mt[...], None
    for i, (dz, fz) in enumerate(zz):
        m_z[i].wait_recv()
        if fz:
            other = mb[i] if other is None else other + mb[i]
        else:
            same = same + mb[i]
    mg[y, zh] = same
    mg[y, 1 - zh] = other
    m_y = [
        send(mg.at[y], mg.at[y], mss.at[13 + dy], mrs.at[13 + dy], dev(dy=dy)) for dy in (2, 1, 3)
    ]

    for copy in r_core:
        copy.wait_recv()
    for p in range(8):
        v = jnp.concatenate([rg[4 * p + q] for q in range(4)], axis=0)
        high, low = split(v)
        rh_v[16 * p : 16 * (p + 1), :] = high
        rl_v[16 * p : 16 * (p + 1), :] = low

    def r3(k):
        where = slice(k * CW, (k + 1) * CW)
        return jnp.concatenate([rh_v[:, where], rh_v[:, where], rl_v[:, where]], axis=0)

    landed(bb_c)
    for k in range(CH):
        where = slice(k * CW, (k + 1) * CW)
        bbar_out[:, where] = bbar_v[:, where] - dot(x3_v[...], r3(k), precision=None)

    def second_axis(k):
        for copy in t_1[k]:
            copy.wait_recv()
        if k == ZK:
            x1[...] = z1[zl] + zr1[0] + zr1[1] + zr1[2]
            return [
                send(x1.at[(x + dx) % NX], xr1.at[dx - 1], xss.at[k, dx - 1], xrs.at[k, dx - 1], dev(dx=dx))
                for dx in (2, 1, 3)
            ]
        n = CUTS[k + 1] - CUTS[k]
        w = pl.ds(0, n)
        v = ts[k, x, :, :n] + xr[k, 0, :, :n] + xr[k, 1, :, :n] + xr[k, 2, :, :n]
        for q in range(NZ):
            zs[k, q, :, :n] = v[4 * q : 4 * q + 4]
        return [
            send(
                zs.at[k, (zl + dz) % NZ, :, w], zr.at[k, dz - 1, :, w],
                zss.at[k, dz - 1], zrs.at[k, dz - 1], dev(dz=dz),
            )
            for dz in range(1, NZ)
        ]

    t_2 = {k: second_axis(k) for k in (0, ZK, 1)}

    for copy in m_y:
        copy.wait_recv()
    parts = []
    for q in range(NY):
        for h in range(NH):
            lanes = slice(64 * h, 64 * h + 64)
            parts.append(jnp.concatenate([mg[q, 0][:, lanes], mg[q, 1][:, lanes]], axis=1))
    mt_full = jnp.concatenate(parts, axis=0)
    mid = dk_v[...] - jnp.where(rows >= order_c, dot(w_v[...], mt_full), 0.0)
    z = dot(uk_v[...], mid)
    q = jnp.where(order_r >= order_c, z, z.T)
    w8 = wk_v[pl.ds(pl.multiple_of(row // 2 * 8, 8), 8), :]
    wq = dot(w8, q)
    a8 = dot(wq, wk_v[...], ((1,), (1,)))
    a4 = jnp.where(core == 0, a8[:4], a8[4:])
    row4 = lax.broadcasted_iota(jnp.int32, (4, 128), 0) + row * 4
    col4 = lax.broadcasted_iota(jnp.int32, (4, 128), 1)
    kda = jnp.where(row4 > col4, a4, jnp.where(row4 == col4, 0.5 * a4, 0.0))
    pick = lax.broadcasted_iota(jnp.int32, (128, 16), 0) == (
        lax.broadcasted_iota(jnp.int32, (128, 16), 1) + col * 16
    )
    kda_out[...] = dot(kda, jnp.where(pick, 1.0, 0.0))

    ap = dot(wq, wpk_v[...], ((1,), (1,)))
    ah, al = split(ap)
    a3 = jnp.concatenate([ah, al, ah], axis=1)
    landed(rb_c)
    for k in range(CH):
        where = slice(k * CW, (k + 1) * CW)
        corr = dot(a3, r3(k), precision=None)
        rbar_v[:, where] = rbar_v[:, where] - jnp.where(core == 0, corr[:4], corr[4:])
    for k in range(NK):
        where, n = slice(CUTS[k], CUTS[k + 1]), CUTS[k + 1] - CUTS[k]
        for copy in t_2[k]:
            copy.wait_recv()
        if k == ZK:
            acc = x1[x] + xr1[0] + xr1[1] + xr1[2]
        else:
            acc = zs[k, zl, :, :n] + zr[k, 0, :, :n] + zr[k, 1, :, :n] + zr[k, 2, :, :n]
        rbar_out[:, where] = rbar_v[:, where] - acc
    end()


def store(cbar_v, bbar_v, kda_v, rbar_v, cbar_hbm, bbar_hbm, kda_hbm, rbar_hbm, sem):
    copies = [
        pltpu.make_async_copy(bbar_v.at[pl.ds(64 * k, 64)], bbar_hbm.at[pl.ds(64 * k, 64)], sem.at[3 + k])
        for k in range(8)
    ]
    copies += [
        pltpu.make_async_copy(cbar_v, cbar_hbm, sem.at[0]),
        pltpu.make_async_copy(kda_v, kda_hbm, sem.at[1]),
        pltpu.make_async_copy(rbar_v, rbar_hbm, sem.at[2]),
    ]
    for copy in copies:
        copy.start()
    for copy in copies:
        copy.wait()


SHAPES = ((16, 512), (512, 2048), (4, 16), (4, 2048))


def body(c_panel, cbar_in, factor, dbar_in, r_panel, rbar_in, b_block, bbar_in):
    vmem = pltpu.VMEM
    sem = pltpu.SemaphoreType.DMA
    anywhere = pl.BlockSpec(memory_space=pl.ANY)
    in_vmem = pl.BlockSpec(memory_space=vmem)
    scratch = [
        vmem((128, 128), F32), vmem((128, 128), F32), vmem((NY, 16, 512), F32), vmem((4, 2048), F32),
        vmem((512, 2048), F32), vmem((512, 2048), F32), vmem((512, 2048), BF16), vmem((512, 2048), BF16),
        vmem((NH, NY, 16, 512), F32), vmem((32, 4, 2048), F32),
        vmem((128, 128), F32), vmem((128, 128), F32), vmem((128, 128), F32),
        vmem((128, 128), F32), vmem((128, 128), F32),
        vmem((512, 384), BF16), vmem((128, 2048), BF16), vmem((128, 2048), BF16),
        vmem((NK, 2, 64, 1024), F32), vmem((NK, 64, 1024), F32), vmem((NK, NX, 16, 1024), F32),
        vmem((NK, NX - 1, 16, 1024), F32),
        vmem((NK, NZ, 4, 1024), F32), vmem((NK, NZ - 1, 4, 1024), F32),
        vmem((NZ, NX, 4, CW), F32), vmem((NZ - 1, NX, 4, CW), F32),
        vmem((NX, 4, CW), F32), vmem((NX - 1, 4, CW), F32),
        vmem((16, 128), F32), vmem((7, 16, 128), F32), vmem((16, 128), F32), vmem((7, 16, 128), F32),
        vmem((NY, NH, 16, 128), F32),
        sem((7,)), sem((CH,)),
        sem((10,)), sem((10,)), sem((19,)), sem((19,)), sem((CH,)), sem((CH,)),
        sem((CH, 3)), sem((CH, 3)), sem((CH, 3)), sem((CH, 3)), sem((17,)), sem((17,)),
    ]
    args = (c_panel.T, cbar_in.T, factor, dbar_in, r_panel, rbar_in, b_block, bbar_in)
    args = [pltpu.with_memory_space_constraint(a, pltpu.HBM) for a in args]
    results = pl.pallas_call(
        kernel,
        out_shape=[vmem(shape, F32) for shape in SHAPES],
        in_specs=[anywhere] * 8,
        out_specs=[in_vmem] * 4,
        scratch_shapes=scratch,
        compiler_params=pltpu.CompilerParams(
            collective_id=0, has_side_effects=True, vmem_limit_bytes=32 * 1024 * 1024
        ),
        name="block_step",
    )(*args)
    results = [pltpu.with_memory_space_constraint(a, vmem) for a in results]
    cbar_t, bbar_out, kda, rbar_out = pl.pallas_call(
        store,
        out_shape=[jax.ShapeDtypeStruct(shape, F32) for shape in SHAPES],
        in_specs=[anywhere] * 4,
        out_specs=[anywhere] * 4,
        scratch_shapes=[sem((11,))],
        compiler_params=pltpu.CompilerParams(vmem_limit_bytes=4 * 1024 * 1024),
        name="store",
    )(*results)
    return cbar_t.T, bbar_out, kda, rbar_out


def solution(mesh):
    spec = P("row", "col")
    in_specs = (spec, spec, P(), P(), spec, spec, spec, spec)
    return jax.shard_map(
        body, mesh=mesh, in_specs=in_specs, out_specs=(spec,) * 4, check_vma=False
    )
```

```python
import jax
import jax.numpy as jnp
from jax import lax
from jax.experimental import pallas as pl
from jax.experimental.pallas import tpu as pltpu
from jax.sharding import PartitionSpec as P

F32 = jnp.float32
BF16 = jnp.bfloat16
HI = lax.Precision.HIGHEST
MESH = pl.DeviceIdType.MESH
NX, NZ, NY, NC, NH = 4, 4, 4, 2, 2
CH = 4
CW = 512
CUTS = (0, 768, 1536, 2048)
NK = 3
ZK = 2


def dot(a, b, contract=((1,), (0,)), precision=HI):
    return lax.dot_general(
        a, b, (contract, ((), ())), precision=precision, preferred_element_type=F32
    )


def split(a):
    high = a.astype(BF16)
    return high, (a - high.astype(F32)).astype(BF16)


def kernel(
    c_hbm, cbar_hbm, l_hbm, d_hbm, r_hbm, rbar_hbm, b_hbm, bbar_hbm,
    cbar_out, bbar_out, kda_out, rbar_out,
    l_v, d_v, cc, rbar_v, b_v, bbar_v, bh_v, bl_v,
    cg, rg, w_v, wk_v, wpk_v, uk_v, dk_v, x3_v, rh_v, rl_v,
    tb, tc, ts, xr, zs, zr, z1, zr1, x1, xr1,
    ms, ma, mt, mb, mg,
    lsem, bsem,
    cgs, cgr, rs, rr, tss, trs, xss, xrs, zss, zrs, mss, mrs,
):
    row, col = lax.axis_index("row"), lax.axis_index("col")
    core, x, zl = row % NC, (row // NC) % NX, row // (NC * NX)
    y, zh = col // NH, col % NH

    def dev(dz=0, dx=0, fc=0, dy=0, fz=0):
        c2 = 1 - core if fc else core
        h2 = 1 - zh if fz else zh
        z2, x2, y2 = (zl + dz) % NZ, (x + dx) % NX, (y + dy) % NY
        return (z2 * (NX * NC) + x2 * NC + c2, y2 * NH + h2)

    xc = [(dx, fc) for dx in range(NX) for fc in range(NC)][1:]
    zz = [(dz, fz) for dz in range(NZ) for fz in range(NH)][1:]
    peers = [dev(dz=dz, fz=fz) for dz, fz in reversed(zz)]
    peers += [dev(dy=dy) for dy in (2, 1, 3)]
    peers += [dev(dx=dx, fc=fc) for dx, fc in xc]

    barrier = pltpu.get_barrier_semaphore()
    for peer in peers:
        pl.semaphore_signal(barrier, inc=1, device_id=peer, device_id_type=MESH)

    pending = []

    def local(src, dst, sem):
        copy = pltpu.make_async_copy(src, dst, sem)
        copy.start()
        pending.append(copy)
        return copy

    def landed(copy):
        copy.wait()
        pending[:] = [other for other in pending if other is not copy]

    sent = []

    def send(src, dst, ssem, rsem, to):
        copy = pltpu.make_async_remote_copy(
            src_ref=src, dst_ref=dst, send_sem=ssem, recv_sem=rsem,
            device_id=to, device_id_type=MESH,
        )
        copy.start()
        sent.append(copy)
        return copy

    def end():
        for copy in pending:
            copy.wait()
        for copy in sent:
            copy.wait_send()

    my_slot = core * (NX * NZ) + x * NZ + zl
    l_c = local(l_hbm, l_v, lsem.at[0])
    cg_c = local(cbar_hbm, cg.at[zh, y], lsem.at[1])
    c_c = local(c_hbm, cc.at[y], lsem.at[2])
    r_c = local(r_hbm, rg.at[my_slot], lsem.at[3])
    d_c = local(d_hbm, d_v, lsem.at[4])
    rb_c = local(rbar_hbm, rbar_v, lsem.at[5])
    b_c = [
        local(b_hbm.at[:, pl.ds(k * CW, CW)], b_v.at[:, pl.ds(k * CW, CW)], bsem.at[k])
        for k in range(CH)
    ]
    bb_c = local(bbar_hbm, bbar_v, lsem.at[6])

    pl.semaphore_wait(barrier, len(peers))

    cz = send(cbar_hbm, cg.at[zh, y], cgs.at[0], cgr.at[0], dev(fz=1))
    cy = [
        send(cbar_hbm, cg.at[zh, y], cgs.at[dy], cgr.at[dy], dev(dy=dy)) for dy in (2, 1, 3)
    ]
    cc_y = [send(c_hbm, cc.at[y], cgs.at[6 + dy], cgr.at[6 + dy], dev(dy=dy)) for dy in (2, 1, 3)]
    rz = [
        send(r_hbm, rg.at[my_slot], rs.at[dz - 1], rr.at[dz - 1], dev(dz=dz))
        for dz in range(1, NZ)
    ]
    r_x = [
        send(r_hbm, rg.at[my_slot], rs.at[2 + dx], rr.at[2 + dx], dev(dx=dx)) for dx in (2, 1, 3)
    ]

    rows = lax.broadcasted_iota(jnp.int32, (128, 128), 0)
    cols = lax.broadcasted_iota(jnp.int32, (128, 128), 1)
    landed(l_c)
    u = l_v[...].T
    eye = rows == cols
    w = jnp.where(eye, 1.0 / jnp.where(eye, u, 1.0), 0.0)
    for s in (1, 2, 4, 8, 16, 32, 64):
        mask = (rows // (2 * s) == cols // (2 * s)) & (rows % (2 * s) < s) & (cols % (2 * s) >= s)
        w = w - dot(dot(w, jnp.where(mask, u, 0.0)), w)
    w_v[...] = w


    cz.wait_recv()
    part = cg.at[1 - zh, y]
    cy2 = [send(part, part, cgs.at[3 + dy], cgr.at[3 + dy], dev(dy=dy)) for dy in (2, 1, 3)]

    for copy in cc_y:
        copy.wait_recv()
    landed(cg_c)
    landed(c_c)
    pt = dot(jnp.concatenate([cg[0, y], cg[1, y]], axis=0), cc[...].reshape(64, 512), ((1,), (1,)))
    ms[...] = jnp.concatenate([pt[:16], pt[16:]], axis=1)
    m_x = [
        send(ms, ma.at[i], mss.at[i], mrs.at[i], dev(dx=dx, fc=fc))
        for i, (dx, fc) in enumerate(xc)
    ]

    for copy in rz:
        copy.wait_recv()
    landed(r_c)

    def group(g):
        return rg.at[pl.ds(core * (NX * NZ) + ((x + g) % NX) * NZ, NZ)]

    for dz in range(1, NZ):
        slot = rg.at[core * (NX * NZ) + x * NZ + (zl + dz) % NZ]
        r_x += [
            send(slot, slot, rs.at[3 * dz + 2 + dx], rr.at[3 * dz + 2 + dx], dev(dx=dx))
            for dx in (2, 1, 3)
        ]
    r_core = [send(group(0), group(0), rs.at[15], rr.at[15], dev(fc=1))]
    order_c = ((cols % 64) // 16 * 2 + cols // 64) * 16 + cols % 16
    wk = dot(w, jnp.where(rows == order_c, 1.0, 0.0))
    wk_v[...] = wk
    order_r = ((rows % 64) // 16 * 2 + rows // 64) * 16 + rows % 16
    uk_v[...] = dot(jnp.where(cols == order_r, 1.0, 0.0), u)
    landed(d_c)
    dk_v[...] = dot(d_v[...], jnp.where(rows == order_c, 1.0, 0.0))
    natural = (rows % 16) // 4 * 32 + (rows // 16) % 4 * 8 + rows // 64 * 4 + rows % 4
    order = jnp.where(cols == natural, 1.0, 0.0)
    wpk = dot(order, wk)
    wpk_v[...] = wpk

    for k in range(CH):
        landed(b_c[k])
        high, low = split(b_v[:, k * CW : (k + 1) * CW])
        bh_v[:, k * CW : (k + 1) * CW] = high
        bl_v[:, k * CW : (k + 1) * CW] = low

    for copy in cy + cy2:
        copy.wait_recv()
    ct = cg[...].reshape(128, 512)
    ctn = dot(wpk, ct)
    nh, nl = split(ctn)
    both = jnp.concatenate([nh, nl], axis=0)

    def chunk(k):
        where, n = slice(CUTS[k], CUTS[k + 1]), CUTS[k + 1] - CUTS[k]
        p = dot(both, bh_v[:, where], precision=None)
        t = p[:128] + p[128:] + dot(nh, bl_v[:, where], precision=None)
        tb[k, 0, :, :n] = t[:64]
        tb[k, 1, :, :n] = t[64:]
        w = pl.ds(0, n)
        return send(tb.at[k, 1 - core, :, w], tc.at[k, :, w], tss.at[k], trs.at[k], dev(fc=1))

    def after_core(k):
        t_core[k].wait_recv()
        n = CUTS[k + 1] - CUTS[k]
        w = pl.ds(0, n)
        v = tb[k, core, :, :n] + tc[k, :, :n]
        if k == ZK:
            for q in range(NX):
                for p in range(NZ):
                    z1[p, q] = v[16 * q + 4 * p : 16 * q + 4 * p + 4]
            return [
                send(z1.at[(zl + dz) % NZ], zr1.at[dz - 1], zss.at[k, dz - 1], zrs.at[k, dz - 1], dev(dz=dz))
                for dz in range(1, NZ)
            ]
        for q in range(NX):
            ts[k, q, :, :n] = v[16 * q : 16 * (q + 1)]
        return [
            send(
                ts.at[k, (x + dx) % NX, :, w], xr.at[k, dx - 1, :, w],
                xss.at[k, dx - 1], xrs.at[k, dx - 1], dev(dx=dx),
            )
            for dx in (2, 1, 3)
        ]

    t_core = [chunk(k) for k in range(NK)]

    total = ms[...]
    for i, copy in enumerate(m_x):
        copy.wait_recv()
        total = total + ma[i]
    mt[...] = total
    m_z = [
        send(mt, mb.at[i], mss.at[7 + i], mrs.at[7 + i], dev(dz=dz, fz=fz))
        for i, (dz, fz) in enumerate(zz)
    ]
    t_1 = [after_core(k) for k in range(NK)]

    for copy in r_x:
        copy.wait_recv()
    for dx in range(1, NX):
        r_core.append(send(group(dx), group(dx), rs.at[15 + dx], rr.at[15 + dx], dev(fc=1)))

    cbar_out[...] = dot(wk_v[pl.ds(pl.multiple_of(col * 16, 16), 16), :], ct)
    cn = ctn.T
    ch, cl = split(cn)
    x3_v[...] = jnp.concatenate([ch, cl, ch], axis=1)

    same, other = mt[...], None
    for i, (dz, fz) in enumerate(zz):
        m_z[i].wait_recv()
        if fz:
            other = mb[i] if other is None else other + mb[i]
        else:
            same = same + mb[i]
    mg[y, zh] = same
    mg[y, 1 - zh] = other
    m_y = [
        send(mg.at[y], mg.at[y], mss.at[13 + dy], mrs.at[13 + dy], dev(dy=dy)) for dy in (2, 1, 3)
    ]

    for copy in r_core:
        copy.wait_recv()
    for p in range(8):
        v = jnp.concatenate([rg[4 * p + q] for q in range(4)], axis=0)
        high, low = split(v)
        rh_v[16 * p : 16 * (p + 1), :] = high
        rl_v[16 * p : 16 * (p + 1), :] = low

    def r3(k):
        where = slice(k * CW, (k + 1) * CW)
        return jnp.concatenate([rh_v[:, where], rh_v[:, where], rl_v[:, where]], axis=0)

    landed(bb_c)
    for k in range(CH):
        where = slice(k * CW, (k + 1) * CW)
        bbar_out[:, where] = bbar_v[:, where] - dot(x3_v[...], r3(k), precision=None)

    def second_axis(k):
        for copy in t_1[k]:
            copy.wait_recv()
        if k == ZK:
            x1[...] = z1[zl] + zr1[0] + zr1[1] + zr1[2]
            return [
                send(x1.at[(x + dx) % NX], xr1.at[dx - 1], xss.at[k, dx - 1], xrs.at[k, dx - 1], dev(dx=dx))
                for dx in (2, 1, 3)
            ]
        n = CUTS[k + 1] - CUTS[k]
        w = pl.ds(0, n)
        v = ts[k, x, :, :n] + xr[k, 0, :, :n] + xr[k, 1, :, :n] + xr[k, 2, :, :n]
        for q in range(NZ):
            zs[k, q, :, :n] = v[4 * q : 4 * q + 4]
        return [
            send(
                zs.at[k, (zl + dz) % NZ, :, w], zr.at[k, dz - 1, :, w],
                zss.at[k, dz - 1], zrs.at[k, dz - 1], dev(dz=dz),
            )
            for dz in range(1, NZ)
        ]

    t_2 = {k: second_axis(k) for k in (0, ZK, 1)}

    for copy in m_y:
        copy.wait_recv()
    parts = []
    for q in range(NY):
        for h in range(NH):
            lanes = slice(64 * h, 64 * h + 64)
            parts.append(jnp.concatenate([mg[q, 0][:, lanes], mg[q, 1][:, lanes]], axis=1))
    mt_full = jnp.concatenate(parts, axis=0)
    mid = dk_v[...] - jnp.where(rows >= order_c, dot(w_v[...], mt_full), 0.0)
    z = dot(uk_v[...], mid)
    q = jnp.where(order_r >= order_c, z, z.T)
    w8 = wk_v[pl.ds(pl.multiple_of(row // 2 * 8, 8), 8), :]
    wq = dot(w8, q)
    a8 = dot(wq, wk_v[...], ((1,), (1,)))
    a4 = jnp.where(core == 0, a8[:4], a8[4:])
    row4 = lax.broadcasted_iota(jnp.int32, (4, 128), 0) + row * 4
    col4 = lax.broadcasted_iota(jnp.int32, (4, 128), 1)
    kda = jnp.where(row4 > col4, a4, jnp.where(row4 == col4, 0.5 * a4, 0.0))
    pick = lax.broadcasted_iota(jnp.int32, (128, 16), 0) == (
        lax.broadcasted_iota(jnp.int32, (128, 16), 1) + col * 16
    )
    kda_out[...] = dot(kda, jnp.where(pick, 1.0, 0.0))

    ap = dot(wq, wpk_v[...], ((1,), (1,)))
    ah, al = split(ap)
    a3 = jnp.concatenate([ah, al, ah], axis=1)
    landed(rb_c)
    for k in range(CH):
        where = slice(k * CW, (k + 1) * CW)
        corr = dot(a3, r3(k), precision=None)
        rbar_v[:, where] = rbar_v[:, where] - jnp.where(core == 0, corr[:4], corr[4:])
    for k in range(NK):
        where, n = slice(CUTS[k], CUTS[k + 1]), CUTS[k + 1] - CUTS[k]
        for copy in t_2[k]:
            copy.wait_recv()
        if k == ZK:
            acc = x1[x] + xr1[0] + xr1[1] + xr1[2]
        else:
            acc = zs[k, zl, :, :n] + zr[k, 0, :, :n] + zr[k, 1, :, :n] + zr[k, 2, :, :n]
        rbar_out[:, where] = rbar_v[:, where] - acc
    end()


def store(cbar_v, bbar_v, kda_v, rbar_v, cbar_hbm, bbar_hbm, kda_hbm, rbar_hbm, sem):
    copies = [
        pltpu.make_async_copy(bbar_v.at[pl.ds(64 * k, 64)], bbar_hbm.at[pl.ds(64 * k, 64)], sem.at[3 + k])
        for k in range(8)
    ]
    copies += [
        pltpu.make_async_copy(cbar_v, cbar_hbm, sem.at[0]),
        pltpu.make_async_copy(kda_v, kda_hbm, sem.at[1]),
        pltpu.make_async_copy(rbar_v, rbar_hbm, sem.at[2]),
    ]
    for copy in copies:
        copy.start()
    for copy in copies:
        copy.wait()


SHAPES = ((16, 512), (512, 2048), (4, 16), (4, 2048))


def body(c_panel, cbar_in, factor, dbar_in, r_panel, rbar_in, b_block, bbar_in):
    vmem = pltpu.VMEM
    sem = pltpu.SemaphoreType.DMA
    anywhere = pl.BlockSpec(memory_space=pl.ANY)
    in_vmem = pl.BlockSpec(memory_space=vmem)
    scratch = [
        vmem((128, 128), F32), vmem((128, 128), F32), vmem((NY, 16, 512), F32), vmem((4, 2048), F32),
        vmem((512, 2048), F32), vmem((512, 2048), F32), vmem((512, 2048), BF16), vmem((512, 2048), BF16),
        vmem((NH, NY, 16, 512), F32), vmem((32, 4, 2048), F32),
        vmem((128, 128), F32), vmem((128, 128), F32), vmem((128, 128), F32),
        vmem((128, 128), F32), vmem((128, 128), F32),
        vmem((512, 384), BF16), vmem((128, 2048), BF16), vmem((128, 2048), BF16),
        vmem((NK, 2, 64, 1024), F32), vmem((NK, 64, 1024), F32), vmem((NK, NX, 16, 1024), F32),
        vmem((NK, NX - 1, 16, 1024), F32),
        vmem((NK, NZ, 4, 1024), F32), vmem((NK, NZ - 1, 4, 1024), F32),
        vmem((NZ, NX, 4, CW), F32), vmem((NZ - 1, NX, 4, CW), F32),
        vmem((NX, 4, CW), F32), vmem((NX - 1, 4, CW), F32),
        vmem((16, 128), F32), vmem((7, 16, 128), F32), vmem((16, 128), F32), vmem((7, 16, 128), F32),
        vmem((NY, NH, 16, 128), F32),
        sem((7,)), sem((CH,)),
        sem((10,)), sem((10,)), sem((19,)), sem((19,)), sem((CH,)), sem((CH,)),
        sem((CH, 3)), sem((CH, 3)), sem((CH, 3)), sem((CH, 3)), sem((17,)), sem((17,)),
    ]
    args = (c_panel.T, cbar_in.T, factor, dbar_in, r_panel, rbar_in, b_block, bbar_in)
    args = [pltpu.with_memory_space_constraint(a, pltpu.HBM) for a in args]
    results = pl.pallas_call(
        kernel,
        out_shape=[vmem(shape, F32) for shape in SHAPES],
        in_specs=[anywhere] * 8,
        out_specs=[in_vmem] * 4,
        scratch_shapes=scratch,
        compiler_params=pltpu.CompilerParams(
            collective_id=0, has_side_effects=True, vmem_limit_bytes=32 * 1024 * 1024
        ),
        name="block_step",
    )(*args)
    results = [pltpu.with_memory_space_constraint(a, vmem) for a in results]
    cbar_t, bbar_out, kda, rbar_out = pl.pallas_call(
        store,
        out_shape=[jax.ShapeDtypeStruct(shape, F32) for shape in SHAPES],
        in_specs=[anywhere] * 4,
        out_specs=[anywhere] * 4,
        scratch_shapes=[sem((11,))],
        compiler_params=pltpu.CompilerParams(vmem_limit_bytes=4 * 1024 * 1024),
        name="store",
    )(*results)
    return cbar_t.T, bbar_out, kda, rbar_out


def solution(mesh):
    spec = P("row", "col")
    in_specs = (spec, spec, P(), P(), spec, spec, spec, spec)
    return jax.shard_map(
        body, mesh=mesh, in_specs=in_specs, out_specs=(spec,) * 4, check_vma=False
    )
```
